128 devices in a mesh: row: 8 (over y, x_hi), col: 16 (over x_lo, z, core).
Axes of the slice: x: 4 (x_hi: 2, x_lo: 2; x = x_hi * 2 + x_lo), y: 4, z: 4, core: 2. Of those that a mesh axis runs over, the one named last changes fastest.
Arguments:
- tokens: bfloat16 [512, 12288], P('col', 'row'), may hold values from -6 to 6
- weight: bfloat16 [12288, 49152], P('row', 'col'), may hold values from -0.0546875 to 0.0546875
- cotangent: bfloat16 [512, 49152], P('row', 'col'), may hold values from -6 to 6
Outputs:
- activated: bfloat16 [512, 49152], P('row', 'col')
- input_grad: bfloat16 [512, 12288], P('col', 'row')
- weight_grad: bfloat16 [12288, 49152], P('row', 'col')
The draws below stay inside these ranges and needn't reach their ends.
All inputs are finite; a program needn't handle non-finite values.
Results may differ from the reference program's by a relative error of at most 0.025.
Values may be sent and summed in bfloat16 or wider, within the bound.
No kernel may reach another device: no remote copies, remote signals or barrier semaphores. Data moves between devices by JAX's collectives and lax.ppermute only.
A program may use at most 128 MiB of HBM per device.

```python
import jax
import jax.numpy as jnp
from jax import lax

D = 12288
FF = 49152
TOKENS = 512
N_ROW = 8
N_COL = 16


def block_scale(rng, dims, shards, smallest, largest):
    factor_of, own = 1.0, jax.random.fold_in(rng, 6)
    for position, blocks in shards:
        heights = jnp.exp(jax.random.uniform(jax.random.fold_in(own, position), (blocks,), jnp.float32, smallest / len(shards), largest / len(shards)))
        factor_of = factor_of * jnp.repeat(heights, dims[position] // blocks).reshape([-1 if axis == position else 1 for axis in range(len(dims))])
    return factor_of


def scatter_about(key, dims, scale, bound, shards=(), kind=jnp.bfloat16):
    values = jax.random.normal(key, dims, jnp.float32) * scale
    if len(shards) > 0:
        values = block_scale(key, dims, shards, -0.22, 0.18) * values
    return jnp.clip(values, min=-bound, max=bound).astype(kind)


def setup_inputs(seed: int = 0) -> dict:
    seeds = jax.random.split(jax.random.key(seed), 4)
    return {
        "tokens": scatter_about(seeds[0], (TOKENS, D), 1.0, 6.0, ((0, 16), (1, 8))),
        "weight": scatter_about(seeds[1], (D, FF), D ** -0.5, 0.0546875, ((0, 8), (1, 16))),
        "cotangent": scatter_about(seeds[2], (TOKENS, FF), 1.0, 6.0, ((0, 8), (1, 16))),
    }


def gelu_parts(pre):
    coeff = 0.7978845608
    inner = coeff * (pre + 0.044715 * pre * pre * pre)
    tval = jnp.tanh(inner)
    value = 0.5 * pre * (1.0 + tval)
    slope = 0.5 * (1.0 + tval) + 0.5 * pre * (1.0 - tval * tval) * coeff * (1.0 + 3.0 * 0.044715 * pre * pre)
    return value, slope


def reference(tokens, weight, cotangent):
    width = D // N_ROW
    preact = jnp.zeros((TOKENS, FF), jnp.float32)
    for block in range(N_ROW):
        part = jnp.dot(tokens[:, block * width:(block + 1) * width], weight[block * width:(block + 1) * width, :], preferred_element_type=jnp.float32)
        rounded = lax.optimization_barrier(part.astype(jnp.bfloat16))
        preact = preact + rounded.astype(jnp.float32)
    value, slope = gelu_parts(preact)
    activated = value.astype(jnp.bfloat16)
    hidden_grad = (cotangent.astype(jnp.float32) * slope).astype(jnp.bfloat16)
    hidden_width = FF // N_COL
    grad_sum = jnp.zeros((TOKENS, D), jnp.float32)
    for block in range(N_COL):
        lower = block * hidden_width
        upper = (block + 1) * hidden_width
        part = lax.dot_general(hidden_grad[:, lower:upper], weight[:, lower:upper], (((1,), (1,)), ((), ())), preferred_element_type=jnp.float32)
        rounded = lax.optimization_barrier(part.astype(jnp.bfloat16))
        grad_sum = grad_sum + rounded.astype(jnp.float32)
    input_grad = grad_sum.astype(jnp.bfloat16)
    weight_grad = jnp.dot(tokens.T, hidden_grad, preferred_element_type=jnp.float32).astype(jnp.bfloat16)
    return activated, input_grad, weight_grad
```

```python
import jax
import jax.numpy as jnp
from jax import lax
from jax.sharding import Mesh
from jax.sharding import PartitionSpec as P

ROW = ("y", "xh")
PLANE = ("xl", "z")


def gelu_parts(pre):
    coeff = 0.7978845608
    inner = coeff * (pre + 0.044715 * pre * pre * pre)
    tval = jnp.tanh(inner)
    value = 0.5 * pre * (1.0 + tval)
    slope = 0.5 * (1.0 + tval) + 0.5 * pre * (1.0 - tval * tval) * coeff * (
        1.0 + 3.0 * 0.044715 * pre * pre
    )
    return (value, slope)


def local(tokens, weight, cotangent):
    rows, width = tokens.shape
    half = width // 2
    mine = lax.all_to_all(tokens, "c", 1, 0, tiled=True)
    spread = jnp.broadcast_to(mine[None], (8, 2 * rows, half)).reshape(16 * rows, half)
    part = lax.all_to_all(spread, PLANE, 0, 0, tiled=True)
    full_tokens = lax.all_gather(part, "c", axis=1, tiled=True)

    partial = jnp.dot(full_tokens, weight, preferred_element_type=jnp.float32).astype(jnp.bfloat16)
    got = lax.all_to_all(partial, ROW, 0, 0, tiled=True)
    block, hidden = cotangent.shape
    preact = jnp.sum(got.reshape(8, block, hidden).astype(jnp.float32), axis=0)
    value, slope = gelu_parts(preact)
    local_grad = (cotangent.astype(jnp.float32) * slope).astype(jnp.bfloat16)
    activated = value.astype(jnp.bfloat16)
    spread = jnp.broadcast_to(local_grad[None], (8, block, hidden)).reshape(8 * block, hidden)
    grad_full = lax.all_to_all(spread, ROW, 0, 0, tiled=True)

    part = lax.dot_general(
        grad_full, weight, (((1,), (1,)), ((), ())), preferred_element_type=jnp.float32
    ).astype(jnp.bfloat16)
    pair = lax.all_to_all(part.reshape(16 * rows, 2, half), "c", 1, 1, tiled=True)
    pair = jnp.sum(pair.astype(jnp.float32), axis=1).astype(jnp.bfloat16)
    got = lax.all_to_all(pair, PLANE, 0, 0, tiled=True)
    total = jnp.sum(got.reshape(8, 2 * rows, half).astype(jnp.float32), axis=0).astype(jnp.bfloat16)
    input_grad = lax.all_to_all(total, "c", 0, 1, tiled=True)

    weight_grad = jnp.dot(full_tokens.T, grad_full, preferred_element_type=jnp.float32).astype(
        jnp.bfloat16
    )
    return (activated, input_grad, weight_grad)


def solution(mesh):
    fine = Mesh(mesh.devices.reshape(4, 2, 2, 4, 2), ("y", "xh", "xl", "z", "c"))
    row, col = P(ROW), ("xl", "z", "c")
    return jax.shard_map(
        local,
        mesh=fine,
        in_specs=(P(col, ROW), P(ROW, col), P(ROW, col)),
        out_specs=(P(ROW, col), P(col, ROW), P(ROW, col)),
        check_vma=False,
    )
```

```python
import functools

import jax
import jax.numpy as jnp
from jax import lax
from jax.experimental import pallas as pl
from jax.experimental.pallas import tpu as pltpu
from jax.sharding import Mesh
from jax.sharding import PartitionSpec as P

N_Y = 4
ROW = ("y", "xh")
PLANE = ("xl", "z")
SWAP = ((0, 1), (1, 0))
LIMIT = 40 * 2**20
F32, BF16 = jnp.float32, jnp.bfloat16
VMEM = pltpu.VMEM


def gelu_parts(pre):
    coeff = 0.7978845608
    inner = coeff * (pre + 0.044715 * pre * pre * pre)
    tval = jnp.tanh(inner)
    value = 0.5 * pre * (1.0 + tval)
    slope = 0.5 * (1.0 + tval) + 0.5 * pre * (1.0 - tval * tval) * coeff * (
        1.0 + 3.0 * 0.044715 * pre * pre
    )
    return (value, slope)


def ahead(array, distance):
    return lax.ppermute(array, "y", [(i, (i + distance) % N_Y) for i in range(N_Y)])


def across(array):
    return lax.ppermute(array, "xh", SWAP)


def block_of(place, distance, side):
    return lax.rem(place[0] + distance, N_Y) * 2 + lax.rem(place[1] + side, 2)


def forward_kernel(pieces, place, tokens, weight, *outs):
    held = outs[-1]
    outs = outs[:-1]
    rows = tokens.shape[1]

    @pl.when(pl.program_id(0) == 0)
    def _():
        for distance in range(N_Y):
            for side in range(2):
                start = (2 * distance + side) * rows
                held[start : start + rows, :] = tokens[block_of(place, distance, side)]

    part = jnp.dot(held[...], weight[...], preferred_element_type=F32).astype(BF16)
    for out, piece in zip(outs, pieces):
        for slot, (distance, side) in enumerate(piece):
            start = (2 * distance + side) * rows
            out[slot * rows : (slot + 1) * rows, :] = part[start : start + rows, :]


def forward(place, tokens, weight, pieces, name):
    blocks, rows, width = tokens.shape
    hidden = weight.shape[1]
    step = 512
    outs = [jax.ShapeDtypeStruct((len(piece) * rows, hidden), BF16) for piece in pieces]
    specs = [pl.BlockSpec((len(piece) * rows, step), lambda i, _: (0, i)) for piece in pieces]
    return pl.pallas_call(
        functools.partial(forward_kernel, pieces),
        out_shape=outs + [jax.ShapeDtypeStruct((blocks * rows, width), BF16)],
        grid_spec=pltpu.PrefetchScalarGridSpec(
            num_scalar_prefetch=1,
            grid=(hidden // step,),
            in_specs=[
                pl.BlockSpec((blocks, rows, width), lambda i, _: (0, 0, 0)),
                pl.BlockSpec((width, step), lambda i, _: (0, i)),
            ],
            out_specs=specs + [pl.BlockSpec((blocks * rows, width), lambda i, _: (0, 0))],
        ),
        compiler_params=pltpu.CompilerParams(vmem_limit_bytes=LIMIT),
        cost_estimate=pl.CostEstimate(
            flops=2 * blocks * rows * width * hidden,
            bytes_accessed=2 * (width * hidden + blocks * rows * (2 * width + hidden)),
            transcendentals=0,
        ),
        name=name,
    )(place, tokens, weight)


def backward_kernel(pieces, place, *refs):
    grads = refs[: len(pieces)]
    weight, out, held = refs[len(pieces) :]
    rows = out.shape[1]

    @pl.when(pl.program_id(0) == 0)
    def _():
        for grad, piece in zip(grads, pieces):
            for slot, (distance, side) in enumerate(piece):
                start = (2 * distance + side) * rows
                held[start : start + rows, :] = grad[slot * rows : (slot + 1) * rows, :]

    part = lax.dot_general(
        held[...], weight[...], (((1,), (1,)), ((), ())), preferred_element_type=F32
    ).astype(BF16)
    for distance in range(N_Y):
        for side in range(2):
            start = (2 * distance + side) * rows
            out[block_of(place, distance, side)] = part[start : start + rows, :]


def backward(place, grads, weight, pieces, name):
    width, hidden = weight.shape
    rows = grads[0].shape[0] // len(pieces[0])
    blocks = 2 * N_Y
    step = 256
    whole = lambda a: pl.BlockSpec(a.shape, lambda i, _: (0, 0))
    return pl.pallas_call(
        functools.partial(backward_kernel, pieces),
        out_shape=[
            jax.ShapeDtypeStruct((blocks, rows, width), BF16),
            jax.ShapeDtypeStruct((blocks * rows, hidden), BF16),
        ],
        grid_spec=pltpu.PrefetchScalarGridSpec(
            num_scalar_prefetch=1,
            grid=(width // step,),
            in_specs=[whole(a) for a in grads]
            + [pl.BlockSpec((step, hidden), lambda i, _: (i, 0))],
            out_specs=[
                pl.BlockSpec((blocks, rows, step), lambda i, _: (0, 0, i)),
                pl.BlockSpec((blocks * rows, hidden), lambda i, _: (0, 0)),
            ],
        ),
        compiler_params=pltpu.CompilerParams(vmem_limit_bytes=LIMIT),
        cost_estimate=pl.CostEstimate(
            flops=2 * blocks * rows * width * hidden,
            bytes_accessed=2 * (width * hidden + blocks * rows * (width + 2 * hidden)),
            transcendentals=0,
        ),
        name=name,
    )(place, *grads, weight)


def weight_grad_kernel(tok_a, tok_b, grad_a, grad_b, out):
    dims = (((0,), (0,)), ((), ()))
    total = lax.dot_general(tok_a[...], grad_a[...], dims, preferred_element_type=F32)
    total += lax.dot_general(tok_b[...], grad_b[...], dims, preferred_element_type=F32)
    out[...] = total.astype(out.dtype)


def weight_grad_of(tok_a, tok_b, grad_a, grad_b):
    rows, width = tok_a.shape
    hidden = grad_a.shape[1]
    step = 512
    whole = pl.BlockSpec((rows, width), lambda i: (0, 0))
    part = pl.BlockSpec((rows, step), lambda i: (0, i))
    return pl.pallas_call(
        weight_grad_kernel,
        grid=(hidden // step,),
        in_specs=[whole, whole, part, part],
        out_specs=pl.BlockSpec((width, step), lambda i: (0, i)),
        out_shape=jax.ShapeDtypeStruct((width, hidden), BF16),
        compiler_params=pltpu.CompilerParams(vmem_limit_bytes=LIMIT),
        cost_estimate=pl.CostEstimate(
            flops=4 * rows * width * hidden,
            bytes_accessed=2 * (width * hidden + 2 * rows * (width + hidden)),
            transcendentals=0,
        ),
        name="weight_grad",
    )(tok_a, tok_b, grad_a, grad_b)


def middle(preact, cot):
    value, slope = gelu_parts(preact)
    return value.astype(BF16), (cot.astype(F32) * slope).astype(BF16)


def local(tokens, weight, cotangent):
    rows, width = tokens.shape
    block, hidden = cotangent.shape
    core = lax.axis_index("c")
    place = jnp.stack([lax.axis_index("y"), lax.axis_index("xh")]).astype(jnp.int32)
    cots = cotangent.reshape(2, rows, hidden)
    cot_own = lax.dynamic_index_in_dim(cots, core, 0, False)
    cot_other = lax.dynamic_index_in_dim(cots, 1 - core, 0, False)
    by_distance = [[(d, 0), (d, 1)] for d in range(N_Y)]
    by_side = [[(d, s) for d in range(N_Y)] for s in range(2)]

    spread = jnp.broadcast_to(tokens[None], (8, rows, width))
    own = lax.all_to_all(spread, PLANE, 0, 0, tiled=True)
    other = lax.ppermute(own, "c", SWAP)

    *parts, tok_own = forward(place, own, weight, by_distance, "forward_own")
    got = [ahead(parts[d], d) for d in (1, 2, 3)]
    *sides, tok_other = forward(place, other, weight, by_side, "forward_other")
    got_side = across(sides[1])

    total = sum((a.astype(F32) for a in got), parts[0].astype(F32))
    got_own = across(total[rows:].astype(BF16))

    pair = (sides[0].astype(F32) + got_side.astype(F32)).reshape(N_Y, rows, hidden)
    got = [ahead(pair[d].astype(BF16), d) for d in (1, 2, 3)]

    act_own, grad_own = middle(total[:rows] + got_own.astype(F32), cot_own)
    near = jnp.concatenate([grad_own] + [ahead(grad_own, -d) for d in (1, 2, 3)], axis=0)
    far = across(near)

    act_other, grad_other = middle(sum((a.astype(F32) for a in got), pair[0]), cot_other)
    both = jnp.concatenate([grad_other, across(grad_other)], axis=0)
    wide = [both] + [ahead(both, -d) for d in (1, 2, 3)]

    back_other, full_other = backward(place, wide, weight, by_distance, "backward_other")
    arrived = lax.ppermute(back_other, "c", SWAP)
    back_own, full_own = backward(place, [near, far], weight, by_side, "backward_own")
    chip = (back_own.astype(F32) + arrived.astype(F32)).astype(BF16)
    got = lax.all_to_all(chip, PLANE, 0, 0, tiled=True)
    input_grad = jnp.sum(got.astype(F32), axis=0).astype(BF16)
    weight_grad = weight_grad_of(tok_own, tok_other, full_own, full_other)
    first = core == 0
    activated = jnp.concatenate(
        [jnp.where(first, act_own, act_other), jnp.where(first, act_other, act_own)], axis=0
    )
    return (activated, input_grad, weight_grad)


def solution(mesh):
    fine = Mesh(mesh.devices.reshape(N_Y, 2, 2, 4, 2), ("y", "xh", "xl", "z", "c"))
    col = ("xl", "z", "c")
    return jax.shard_map(
        local,
        mesh=fine,
        in_specs=(P(col, ROW), P(ROW, col), P(ROW, col)),
        out_specs=(P(ROW, col), P(col, ROW), P(ROW, col)),
        check_vma=False,
    )
```

```python
import functools

import jax
import jax.numpy as jnp
from jax import lax
from jax.experimental import pallas as pl
from jax.experimental.pallas import tpu as pltpu
from jax.sharding import Mesh
from jax.sharding import PartitionSpec as P

N_Y = 4
ROW = ("y", "xh")
PLANE = ("xl", "z")
SWAP = ((0, 1), (1, 0))
MIB = 2**20
STEP = 512
F32, BF16 = jnp.float32, jnp.bfloat16
ON_CHIP = pl.BlockSpec(memory_space=pltpu.VMEM)
SCALARS = pl.BlockSpec(memory_space=pltpu.SMEM)
ANYWHERE = pl.BlockSpec(memory_space=pl.ANY)
IN_HBM = pl.BlockSpec(memory_space=pltpu.HBM)
BY_DISTANCE = tuple(((d, 0), (d, 1)) for d in range(N_Y))
BY_SIDE = tuple(tuple((d, s) for d in range(N_Y)) for s in range(2))


def gelu_parts(pre):
    coeff = 0.7978845608
    inner = coeff * (pre + 0.044715 * pre * pre * pre)
    tval = jnp.tanh(inner)
    value = 0.5 * pre * (1.0 + tval)
    slope = 0.5 * (1.0 + tval) + 0.5 * pre * (1.0 - tval * tval) * coeff * (
        1.0 + 3.0 * 0.044715 * pre * pre
    )
    return (value, slope)


def ahead(array, distance):
    return lax.ppermute(array, "y", [(i, (i + distance) % N_Y) for i in range(N_Y)])


def across(array):
    return lax.ppermute(array, "xh", SWAP)


def other_core(array):
    return lax.ppermute(array, "c", SWAP)


def after(value, *others):
    return lax.optimization_barrier((value, others))[0]


def block_of(place, distance, side):
    return lax.rem(place[0] + distance, N_Y) * 2 + lax.rem(place[1] + side, 2)


def tiles_of(width):
    return [slice(i, i + STEP) for i in range(0, width, STEP)]


def call(kernel, name, outs, ins, args, flops, size, transcendentals=0, scratch=(), limit=16, aliases=None):
    return pl.pallas_call(
        kernel,
        out_shape=[jax.ShapeDtypeStruct(shape, dtype) for shape, dtype, _ in outs],
        in_specs=ins,
        out_specs=[spec for _, _, spec in outs],
        scratch_shapes=list(scratch),
        input_output_aliases=aliases or {},
        compiler_params=pltpu.CompilerParams(vmem_limit_bytes=limit * MIB),
        cost_estimate=pl.CostEstimate(
            flops=flops, bytes_accessed=size, transcendentals=transcendentals
        ),
        name=name,
    )(*args)


def load_kernel(offset, source, out, sem):
    columns = slice(offset, offset + out.shape[1])
    copy = pltpu.make_async_copy(source.at[:, columns], out, sem)
    copy.start()
    copy.wait()


def load(weight, part, name):
    width = weight.shape[0]
    count = part.stop - part.start
    return call(
        functools.partial(load_kernel, part.start),
        name,
        [((width, count), BF16, ON_CHIP)],
        [ANYWHERE],
        [weight],
        flops=0,
        size=4 * width * count,
        scratch=[pltpu.SemaphoreType.DMA(())],
        limit=48,
    )[0]


def row_of(rows, core, distance, side):
    return (core * 2 * N_Y + 2 * distance + side) * rows


def place_tokens(place, tokens, held, core):
    rows = tokens.shape[1]
    for distance in range(N_Y):
        for side in range(2):
            start = row_of(rows, core, distance, side)
            held[start : start + rows, :] = tokens[block_of(place, distance, side)]


def put_sides(part, outs, columns, rows, core):
    for side, out in enumerate(outs):
        for distance in range(N_Y):
            start, to = (2 * distance + side) * rows, (core * N_Y + distance) * rows
            out[to : to + rows, columns] = part[start : start + rows, :]


def tile_copy(weight, offset, tiles, sems, i):
    columns = pl.ds(pl.multiple_of(offset + i * STEP, STEP), STEP)
    return pltpu.make_async_copy(weight.at[:, columns], tiles.at[i], sems.at[i])


def forward_side_kernel(place, own, other, weight, toks, first, second):
    rows = own.shape[1]
    place_tokens(place, own, toks, 0)
    place_tokens(place, other, toks, 1)

    def body(i, carry):
        columns = pl.ds(pl.multiple_of(i * STEP, STEP), STEP)
        part = jnp.dot(toks[...], weight[:, columns], preferred_element_type=F32).astype(BF16)
        for core in range(2):
            start = row_of(rows, core, 0, 0)
            put_sides(part[start : start + 2 * N_Y * rows], (first, second), columns, rows, core)
        return carry

    lax.fori_loop(0, weight.shape[1] // STEP, body, 0)


def forward_side(place, own, other, weight):
    blocks, rows, width = own.shape
    count = weight.shape[1]
    side = ((blocks * rows, count), BF16, ON_CHIP)
    return call(
        forward_side_kernel,
        "forward_side",
        [((2 * blocks * rows, width), BF16, ON_CHIP), side, side],
        [SCALARS] + [ON_CHIP] * 3,
        [place, own, other, weight],
        flops=4 * blocks * rows * width * count,
        size=2 * width * count,
    )


def forward_distance_kernel(offset, toks, weight, *refs):
    *outs, tiles, sems = refs
    steps = tiles.shape[0]
    rows = outs[0].shape[0] // 4
    for i in range(steps):
        tile_copy(weight, offset, tiles, sems, i).start()

    def body(i, carry):
        tile_copy(weight, offset, tiles, sems, i).wait()
        columns = pl.ds(pl.multiple_of(i * STEP, STEP), STEP)
        part = jnp.dot(toks[...], tiles[i], preferred_element_type=F32).astype(BF16)
        for distance, out in enumerate(outs):
            for side in range(2):
                for core in range(2):
                    start, to = row_of(rows, core, distance, side), (2 * side + core) * rows
                    out[to : to + rows, columns] = part[start : start + rows, :]
        return carry

    lax.fori_loop(0, steps, body, 0)


def forward_distance(toks, weight, part):
    tokens, width = toks.shape
    count = part.stop - part.start
    return call(
        functools.partial(forward_distance_kernel, part.start),
        "forward_distance",
        [((tokens // N_Y, count), BF16, ON_CHIP)] * N_Y,
        [ON_CHIP, ANYWHERE],
        [toks, weight],
        flops=2 * tokens * width * count,
        size=2 * width * count,
        scratch=[
            pltpu.VMEM((count // STEP, width, STEP), BF16),
            pltpu.SemaphoreType.DMA((count // STEP,)),
        ],
        limit=48,
    )


def assemble(grads, pieces, held, core):
    rows = held.shape[0] // (2 * N_Y)
    for grad, piece in zip(grads, pieces):
        for slot, (distance, side) in enumerate(piece):
            start, at = (2 * distance + side) * rows, (2 * slot + core) * rows
            held[start : start + rows, :] = grad[at : at + rows, :]


def times_weight(grad, weight, columns):
    return lax.dot_general(
        grad, weight[columns, :], (((1,), (1,)), ((), ())), preferred_element_type=F32
    )


def backward_first_kernel(pieces, *refs):
    grads = refs[: len(pieces)]
    weight, out, full, held, sem = refs[len(pieces) :]
    half = held.shape[0] // 2
    for core in range(2):
        assemble(grads, pieces, held.at[core * half : (core + 1) * half], core)
    copy = pltpu.make_async_copy(held, full, sem)
    copy.start()

    def body(i, carry):
        columns = pl.ds(pl.multiple_of(i * STEP, STEP), STEP)
        out[:, columns] = times_weight(held[...], weight, columns)
        return carry

    lax.fori_loop(0, weight.shape[0] // STEP, body, 0)
    copy.wait()


def backward_first(grads, weight, pieces):
    width, hidden = weight.shape
    count = sum(grad.shape[0] for grad in grads)
    return call(
        functools.partial(backward_first_kernel, pieces),
        "backward_first",
        [((count, width), F32, ON_CHIP), ((count, hidden), BF16, IN_HBM)],
        [ON_CHIP] * (len(grads) + 1),
        [*grads, weight],
        flops=2 * count * width * hidden,
        size=2 * width * hidden,
        scratch=[pltpu.VMEM((count, hidden), BF16), pltpu.SemaphoreType.DMA(())],
    )


def backward_last_kernel(pieces, core, place, *refs):
    grads = refs[: len(pieces)]
    weight, begun, out, full, held, sem = refs[len(pieces) :]
    assemble(grads, pieces, held, core)
    copy = pltpu.make_async_copy(held, full, sem)
    copy.start()
    rows = out.shape[1]
    half = slice(core * 2 * N_Y * rows, (core + 1) * 2 * N_Y * rows)

    def body(i, carry):
        columns = pl.ds(pl.multiple_of(i * STEP, STEP), STEP)
        part = (begun[half, columns] + times_weight(held[...], weight, columns)).astype(BF16)
        for distance in range(N_Y):
            for side in range(2):
                start = (2 * distance + side) * rows
                out[block_of(place, distance, side), :, columns] = part[start : start + rows, :]
        return carry

    lax.fori_loop(0, weight.shape[0] // STEP, body, 0)
    copy.wait()


def backward_last(place, grads, weight, begun, pieces, core, name):
    width, hidden = weight.shape
    count = begun.shape[0] // 2
    return call(
        functools.partial(backward_last_kernel, pieces, core),
        name,
        [((2 * N_Y, count // (2 * N_Y), width), BF16, ON_CHIP), ((count, hidden), BF16, IN_HBM)],
        [SCALARS] + [ON_CHIP] * (len(grads) + 2),
        [place, *grads, weight, begun],
        flops=2 * count * width * hidden,
        size=2 * width * hidden,
        scratch=[pltpu.VMEM((count, hidden), BF16), pltpu.SemaphoreType.DMA(())],
    )


def add_kernel(mine, got, out):
    for block in range(out.shape[0]):
        out[block] = (mine[block].astype(F32) + got[block].astype(F32)).astype(BF16)


def turn_kernel(tok, out, held, sem):
    held[...] = tok[...].T
    copy = pltpu.make_async_copy(held, out, sem)
    copy.start()
    copy.wait()


def turn(tok):
    rows, width = tok.shape
    return call(
        turn_kernel,
        "turn_tokens",
        [((width, rows), BF16, IN_HBM)],
        [ON_CHIP],
        [tok],
        flops=0,
        size=4 * rows * width,
        scratch=[pltpu.VMEM((width, rows), BF16), pltpu.SemaphoreType.DMA(())],
    )[0]


def weight_grad_kernel(corners, *refs):
    turned, *grads = refs[: len(corners) + 1]
    out, held_turned, held, tiles, sems = refs[len(corners) + 1 :]
    step = tiles.shape[2]
    steps = held.shape[1] // step
    loads = [pltpu.make_async_copy(turned, held_turned, sems.at[2])]
    for i, (grad, (row, column)) in enumerate(zip(grads, corners)):
        rows, columns = slice(row, row + grad.shape[0]), slice(column, column + grad.shape[1])
        loads.append(pltpu.make_async_copy(grad, held.at[rows, columns], sems.at[3 + i]))
    for load in loads:
        load.start()
    for load in loads:
        load.wait()

    def copy(i):
        columns = pl.ds(pl.multiple_of(i * step, step), step)
        slot = lax.rem(i, 2)
        return pltpu.make_async_copy(tiles.at[slot], out.at[:, columns], sems.at[slot])

    def body(i, carry):
        columns = pl.ds(pl.multiple_of(i * step, step), step)

        @pl.when(i >= 2)
        def _():
            copy(i - 2).wait()

        total = jnp.dot(held_turned[...], held[:, columns], preferred_element_type=F32)
        tiles[lax.rem(i, 2)] = total.astype(BF16)
        copy(i).start()
        return carry

    lax.fori_loop(0, steps, body, 0)
    copy(steps - 2).wait()
    copy(steps - 1).wait()


def weight_grad_of(turned, grads, corners, hidden):
    width, rows = turned.shape
    return call(
        functools.partial(weight_grad_kernel, corners),
        "weight_grad",
        [((width, hidden), BF16, IN_HBM)],
        [ANYWHERE] * (1 + len(grads)),
        [turned, *grads],
        flops=2 * rows * width * hidden,
        size=2 * width * hidden,
        scratch=[
            pltpu.VMEM(turned.shape, BF16),
            pltpu.VMEM((rows, hidden), BF16),
            pltpu.VMEM((2, width, STEP), BF16),
            pltpu.SemaphoreType.DMA((3 + len(grads),)),
        ],
        limit=56,
    )[0]


def sum_distance_kernel(mine, got_1, got_2, got_3, near, far):
    rows = near.shape[0]
    for columns in tiles_of(near.shape[1]):
        total = mine[:, columns].astype(F32)
        for got in (got_1, got_2, got_3):
            total += got[:, columns].astype(F32)
        near[:, columns] = total[:rows]
        far[:, columns] = total[rows:].astype(BF16)


def sum_side_kernel(mine, got, *outs):
    rows = outs[0].shape[0] // 2
    for columns in tiles_of(mine.shape[1]):
        for distance, out in enumerate(outs):
            for core in range(2):
                start = (core * N_Y + distance) * rows
                block = slice(start, start + rows)
                total = mine[block, columns].astype(F32) + got[block, columns].astype(F32)
                out[core * rows : (core + 1) * rows, columns] = total.astype(out.dtype)


def gelu_kernel(offset, place, *refs):
    terms = refs[:-3]
    cot, act, grad = refs[-3:]
    rows = act.shape[0] // 2
    for side in range(2):
        core = lax.rem(place[2] + side, 2)
        block = slice(side * rows, (side + 1) * rows)
        absolute = pl.ds(pl.multiple_of(core * rows, rows), rows)
        for columns in tiles_of(act.shape[1]):
            pre = terms[0][block, columns].astype(F32)
            for term in terms[1:]:
                pre += term[block, columns].astype(F32)
            value, slope = gelu_parts(pre)
            act[absolute, columns] = value.astype(BF16)
            from_cot = slice(offset + columns.start, offset + columns.stop)
            grad[block, columns] = (cot[absolute, from_cot].astype(F32) * slope).astype(BF16)


def gelu_step(place, terms, cot, offset, name):
    shape = terms[0].shape
    size = shape[0] * shape[1]
    return call(
        functools.partial(gelu_kernel, offset),
        name,
        [(shape, BF16, ON_CHIP), (shape, BF16, ON_CHIP)],
        [SCALARS] + [ON_CHIP] * (len(terms) + 1),
        [place, *terms, cot],
        flops=40 * size,
        size=8 * size,
        transcendentals=size,
    )


def last_sum_kernel(got, out):
    for columns in tiles_of(out.shape[1]):
        total = got[0, :, columns].astype(F32)
        for i in range(1, got.shape[0]):
            total += got[i, :, columns].astype(F32)
        out[:, columns] = total.astype(BF16)


def local(tokens, weight, cotangent):
    rows, width = tokens.shape
    block, hidden = cotangent.shape
    cut = hidden // 2
    part_a, part_b = slice(0, cut), slice(cut, hidden)
    small_a, small_b = (block, cut), (block, hidden - cut)
    place = jnp.stack([lax.axis_index(a) for a in ("y", "xh", "c")]).astype(jnp.int32)

    spread = jnp.broadcast_to(tokens[None], (8, rows, width))
    own = lax.all_to_all(spread, PLANE, 0, 0, tiled=True)
    other = other_core(own)

    held = load(after(weight, own), part_b, "load_forward")
    toks, *sides = forward_side(place, own, other, held)
    got_side = across(sides[1])
    parts = forward_distance(toks, weight, part_a)
    got_a = [ahead(parts[d], d) for d in (1, 2, 3)]
    got_side = after(got_side, parts[0])
    kept, *sent = call(
        sum_side_kernel,
        "sum_b",
        [(small_b, F32 if d == 0 else BF16, ON_CHIP) for d in range(N_Y)],
        [ON_CHIP] * 2,
        [sides[0], got_side],
        flops=8 * block * hidden,
        size=16 * block * hidden,
    )
    got_b = [ahead(sent[d - 1], d) for d in (1, 2, 3)]
    got_a = after(got_a, sent[0])
    near, far = call(
        sum_distance_kernel,
        "sum_a",
        [(small_a, F32, ON_CHIP), (small_a, BF16, ON_CHIP)],
        [ON_CHIP] * 4,
        [parts[0], *got_a],
        flops=8 * block * hidden,
        size=16 * block * hidden,
    )
    got_far = across(far)

    act_b, grad_b = gelu_step(place, [kept, *got_b], cotangent, cut, "gelu_b")
    grad_b_far = across(grad_b)
    got_far = after(got_far, grad_b)
    act_a, grad_a = gelu_step(place, [near, got_far], cotangent, 0, "gelu_a")
    by_y = [ahead(grad_a, -d) for d in (1, 2, 3)]
    both = jnp.concatenate([grad_b, grad_b_far], axis=0)
    wide = [ahead(both, -d) for d in (1, 2, 3)]
    by_y = jnp.concatenate([grad_a] + after(by_y, both), axis=0)
    by_y_far = across(by_y)
    late, toks = after((weight, toks), by_y)
    held_a, held_b = load(late, part_a, "load_a"), load(late, part_b, "load_b")
    turned = turn(toks)
    activated = jnp.concatenate([act_a, act_b], axis=1)

    by_y_far = after(by_y_far, held_a, held_b, turned, activated)
    begun, full_a = backward_first([by_y, by_y_far], held_a, BY_SIDE)
    wide = [both, *after(wide, begun)]
    theirs, full_theirs = backward_last(place, wide, held_b, begun, BY_DISTANCE, 1, "backward_other")
    arrived = other_core(theirs)
    wide = after(wide, theirs)
    mine, full_mine = backward_last(place, wide, held_b, begun, BY_DISTANCE, 0, "backward_own")
    (chip,) = call(
        add_kernel,
        "chip_sum",
        [(mine.shape, BF16, ON_CHIP)],
        [ON_CHIP] * 2,
        [mine, arrived],
        flops=mine.size,
        size=6 * mine.size,
    )
    last = lax.all_to_all(chip, PLANE, 0, 0, tiled=True)
    full_mine = after(full_mine, chip)
    corners = [(0, 0), (0, cut), (8 * rows, cut)]
    weight_grad = weight_grad_of(turned, [full_a, full_mine, full_theirs], corners, hidden)
    (input_grad,) = call(
        last_sum_kernel,
        "last_sum",
        [((rows, width), BF16, ON_CHIP)],
        [ON_CHIP],
        [last],
        flops=8 * rows * width,
        size=16 * rows * width,
    )
    return (activated, input_grad, weight_grad)


def solution(mesh):
    fine = Mesh(mesh.devices.reshape(N_Y, 2, 2, 4, 2), ("y", "xh", "xl", "z", "c"))
    col = ("xl", "z", "c")
    return jax.shard_map(
        local,
        mesh=fine,
        in_specs=(P(col, ROW), P(ROW, col), P(ROW, col)),
        out_specs=(P(ROW, col), P(col, ROW), P(ROW, col)),
        check_vma=False,
    )
```

```python
import functools

import jax
import jax.numpy as jnp
from jax import lax
from jax.experimental import pallas as pl
from jax.experimental.pallas import tpu as pltpu
from jax.sharding import Mesh
from jax.sharding import PartitionSpec as P

N_Y = 4
ROW = ("y", "xh")
PLANE = ("xl", "z")
SWAP = ((0, 1), (1, 0))
MIB = 2**20
STEP = 512
F32, BF16 = jnp.float32, jnp.bfloat16
ON_CHIP = pl.BlockSpec(memory_space=pltpu.VMEM)
SCALARS = pl.BlockSpec(memory_space=pltpu.SMEM)
ANYWHERE = pl.BlockSpec(memory_space=pl.ANY)
IN_HBM = pl.BlockSpec(memory_space=pltpu.HBM)
BY_DISTANCE = tuple(((d, 0), (d, 1)) for d in range(N_Y))
BY_SIDE = tuple(tuple((d, s) for d in range(N_Y)) for s in range(2))


def gelu_parts(pre):
    coeff = 0.7978845608
    inner = coeff * (pre + 0.044715 * pre * pre * pre)
    tval = jnp.tanh(inner)
    value = 0.5 * pre * (1.0 + tval)
    slope = 0.5 * (1.0 + tval) + 0.5 * pre * (1.0 - tval * tval) * coeff * (
        1.0 + 3.0 * 0.044715 * pre * pre
    )
    return (value, slope)


def ahead(array, distance):
    return lax.ppermute(array, "y", [(i, (i + distance) % N_Y) for i in range(N_Y)])


def across(array):
    return lax.ppermute(array, "xh", SWAP)


def other_core(array):
    return lax.ppermute(array, "c", SWAP)


def after(value, *others):
    return lax.optimization_barrier((value, others))[0]


def block_of(place, distance, side):
    return lax.rem(place[0] + distance, N_Y) * 2 + lax.rem(place[1] + side, 2)


def tiles_of(width):
    return [slice(i, i + STEP) for i in range(0, width, STEP)]


def call(kernel, name, outs, ins, args, flops, size, transcendentals=0, scratch=(), limit=16, aliases=None):
    return pl.pallas_call(
        kernel,
        out_shape=[jax.ShapeDtypeStruct(shape, dtype) for shape, dtype, _ in outs],
        in_specs=ins,
        out_specs=[spec for _, _, spec in outs],
        scratch_shapes=list(scratch),
        input_output_aliases=aliases or {},
        compiler_params=pltpu.CompilerParams(vmem_limit_bytes=limit * MIB),
        cost_estimate=pl.CostEstimate(
            flops=flops, bytes_accessed=size, transcendentals=transcendentals
        ),
        name=name,
    )(*args)


def load_kernel(offset, source, out, sem):
    columns = slice(offset, offset + out.shape[1])
    copy = pltpu.make_async_copy(source.at[:, columns], out, sem)
    copy.start()
    copy.wait()


def load(weight, part, name):
    width = weight.shape[0]
    count = part.stop - part.start
    return call(
        functools.partial(load_kernel, part.start),
        name,
        [((width, count), BF16, ON_CHIP)],
        [ANYWHERE],
        [weight],
        flops=0,
        size=4 * width * count,
        scratch=[pltpu.SemaphoreType.DMA(())],
        limit=48,
    )[0]


def row_of(rows, core, distance, side):
    return (core * 2 * N_Y + 2 * distance + side) * rows


def place_tokens(place, tokens, held, core):
    rows = tokens.shape[1]
    for distance in range(N_Y):
        for side in range(2):
            start = row_of(rows, core, distance, side)
            held[start : start + rows, :] = tokens[block_of(place, distance, side)]


def put_sides(part, outs, columns, rows, core):
    for side, out in enumerate(outs):
        for distance in range(N_Y):
            start, to = (2 * distance + side) * rows, (core * N_Y + distance) * rows
            out[to : to + rows, columns] = part[start : start + rows, :]


def tile_copy(weight, offset, tiles, sems, i):
    columns = pl.ds(pl.multiple_of(offset + i * STEP, STEP), STEP)
    return pltpu.make_async_copy(weight.at[:, columns], tiles.at[i], sems.at[i])


def forward_side_kernel(place, own, other, weight, toks, first, second):
    rows = own.shape[1]
    place_tokens(place, own, toks, 0)
    place_tokens(place, other, toks, 1)

    def body(i, carry):
        columns = pl.ds(pl.multiple_of(i * STEP, STEP), STEP)
        part = jnp.dot(toks[...], weight[:, columns], preferred_element_type=F32).astype(BF16)
        for core in range(2):
            start = row_of(rows, core, 0, 0)
            put_sides(part[start : start + 2 * N_Y * rows], (first, second), columns, rows, core)
        return carry

    lax.fori_loop(0, weight.shape[1] // STEP, body, 0)


def forward_side(place, own, other, weight):
    blocks, rows, width = own.shape
    count = weight.shape[1]
    side = ((blocks * rows, count), BF16, ON_CHIP)
    return call(
        forward_side_kernel,
        "forward_side",
        [((2 * blocks * rows, width), BF16, ON_CHIP), side, side],
        [SCALARS] + [ON_CHIP] * 3,
        [place, own, other, weight],
        flops=4 * blocks * rows * width * count,
        size=2 * width * count,
    )


def forward_distance_kernel(offset, toks, weight, *refs):
    *outs, tiles, sems = refs
    steps = tiles.shape[0]
    rows = outs[0].shape[0] // 4
    for i in range(steps):
        tile_copy(weight, offset, tiles, sems, i).start()

    def body(i, carry):
        tile_copy(weight, offset, tiles, sems, i).wait()
        columns = pl.ds(pl.multiple_of(i * STEP, STEP), STEP)
        part = jnp.dot(toks[...], tiles[i], preferred_element_type=F32).astype(BF16)
        for distance, out in enumerate(outs):
            for side in range(2):
                for core in range(2):
                    start, to = row_of(rows, core, distance, side), (2 * side + core) * rows
                    out[to : to + rows, columns] = part[start : start + rows, :]
        return carry

    lax.fori_loop(0, steps, body, 0)


def forward_distance(toks, weight, part):
    tokens, width = toks.shape
    count = part.stop - part.start
    return call(
        functools.partial(forward_distance_kernel, part.start),
        "forward_distance",
        [((tokens // N_Y, count), BF16, ON_CHIP)] * N_Y,
        [ON_CHIP, ANYWHERE],
        [toks, weight],
        flops=2 * tokens * width * count,
        size=2 * width * count,
        scratch=[
            pltpu.VMEM((count // STEP, width, STEP), BF16),
            pltpu.SemaphoreType.DMA((count // STEP,)),
        ],
        limit=48,
    )


def assemble(grads, pieces, held, core):
    rows = held.shape[0] // (2 * N_Y)
    for grad, piece in zip(grads, pieces):
        for slot, (distance, side) in enumerate(piece):
            start, at = (2 * distance + side) * rows, (2 * slot + core) * rows
            held[start : start + rows, :] = grad[at : at + rows, :]


def times_weight(grad, weight, columns):
    return lax.dot_general(
        grad, weight[columns, :], (((1,), (1,)), ((), ())), preferred_element_type=F32
    )


def backward_first_kernel(pieces, *refs):
    grads = refs[: len(pieces)]
    weight, out, held = refs[len(pieces) :]
    half = held.shape[0] // 2
    for core in range(2):
        assemble(grads, pieces, held.at[core * half : (core + 1) * half], core)

    def body(i, carry):
        columns = pl.ds(pl.multiple_of(i * STEP, STEP), STEP)
        out[:, columns] = times_weight(held[...], weight, columns)
        return carry

    lax.fori_loop(0, weight.shape[0] // STEP, body, 0)


def backward_first(grads, weight, pieces):
    width, hidden = weight.shape
    count = sum(grad.shape[0] for grad in grads)
    return call(
        functools.partial(backward_first_kernel, pieces),
        "backward_first",
        [((count, width), F32, ON_CHIP)],
        [ON_CHIP] * (len(grads) + 1),
        [*grads, weight],
        flops=2 * count * width * hidden,
        size=2 * width * hidden,
        scratch=[pltpu.VMEM((count, hidden), BF16)],
    )[0]


def backward_last_kernel(pieces, core, place, *refs):
    grads = refs[: len(pieces)]
    weight, begun, out, held = refs[len(pieces) :]
    assemble(grads, pieces, held, core)
    rows = out.shape[1]
    half = slice(core * 2 * N_Y * rows, (core + 1) * 2 * N_Y * rows)

    def body(i, carry):
        columns = pl.ds(pl.multiple_of(i * STEP, STEP), STEP)
        part = (begun[half, columns] + times_weight(held[...], weight, columns)).astype(BF16)
        for distance in range(N_Y):
            for side in range(2):
                start = (2 * distance + side) * rows
                out[block_of(place, distance, side), :, columns] = part[start : start + rows, :]
        return carry

    lax.fori_loop(0, weight.shape[0] // STEP, body, 0)


def backward_last(place, grads, weight, begun, pieces, core, name):
    width, hidden = weight.shape
    count = begun.shape[0] // 2
    return call(
        functools.partial(backward_last_kernel, pieces, core),
        name,
        [((2 * N_Y, count // (2 * N_Y), width), BF16, ON_CHIP)],
        [SCALARS] + [ON_CHIP] * (len(grads) + 2),
        [place, *grads, weight, begun],
        flops=2 * count * width * hidden,
        size=2 * width * hidden,
        scratch=[pltpu.VMEM((count, hidden), BF16)],
    )[0]


def add_kernel(mine, got, out):
    for block in range(out.shape[0]):
        out[block] = (mine[block].astype(F32) + got[block].astype(F32)).astype(BF16)


def turn_kernel(tok, out, held, sem):
    held[...] = tok[...].T
    copy = pltpu.make_async_copy(held, out, sem)
    copy.start()
    copy.wait()


def turn(tok):
    rows, width = tok.shape
    return call(
        turn_kernel,
        "turn_tokens",
        [((width, rows), BF16, IN_HBM)],
        [ON_CHIP],
        [tok],
        flops=0,
        size=4 * rows * width,
        scratch=[pltpu.VMEM((width, rows), BF16), pltpu.SemaphoreType.DMA(())],
    )[0]


def weight_grad_kernel(pieces, offsets, *refs):
    turned, *grads = refs[: len(pieces) + 1]
    out, held_turned, held, tiles, sems, load_sems = refs[len(pieces) + 1 :]
    step = tiles.shape[2]
    steps = held.shape[1] // step
    rows = held.shape[0] // (4 * N_Y)
    loads = [pltpu.make_async_copy(turned, held_turned, load_sems.at[0])]
    for grad, piece, offset in zip(grads, pieces, offsets):
        columns = slice(offset, offset + grad.shape[1])
        for slot, (distance, side) in enumerate(piece):
            for core in range(2):
                start, at = row_of(rows, core, distance, side), (2 * slot + core) * rows
                loads.append(
                    pltpu.make_async_copy(
                        grad.at[at : at + rows, :],
                        held.at[start : start + rows, columns],
                        load_sems.at[len(loads)],
                    )
                )
    for load in loads:
        load.start()
    for load in loads:
        load.wait()

    def copy(i):
        columns = pl.ds(pl.multiple_of(i * step, step), step)
        slot = lax.rem(i, 2)
        return pltpu.make_async_copy(tiles.at[slot], out.at[:, columns], sems.at[slot])

    def body(i, carry):
        columns = pl.ds(pl.multiple_of(i * step, step), step)

        @pl.when(i >= 2)
        def _():
            copy(i - 2).wait()

        total = jnp.dot(held_turned[...], held[:, columns], preferred_element_type=F32)
        tiles[lax.rem(i, 2)] = total.astype(BF16)
        copy(i).start()
        return carry

    lax.fori_loop(0, steps, body, 0)
    copy(steps - 2).wait()
    copy(steps - 1).wait()


def weight_grad_of(turned, grads, pieces, offsets, hidden):
    width, rows = turned.shape
    return call(
        functools.partial(weight_grad_kernel, pieces, offsets),
        "weight_grad",
        [((width, hidden), BF16, IN_HBM)],
        [ANYWHERE] * (1 + len(grads)),
        [turned, *grads],
        flops=2 * rows * width * hidden,
        size=2 * width * hidden,
        scratch=[
            pltpu.VMEM(turned.shape, BF16),
            pltpu.VMEM((rows, hidden), BF16),
            pltpu.VMEM((2, width, STEP), BF16),
            pltpu.SemaphoreType.DMA((2,)),
            pltpu.SemaphoreType.DMA((1 + 2 * sum(len(piece) for piece in pieces),)),
        ],
        limit=56,
    )[0]


def sum_distance_kernel(mine, got_1, got_2, got_3, near, far):
    rows = near.shape[0]
    for columns in tiles_of(near.shape[1]):
        total = mine[:, columns].astype(F32)
        for got in (got_1, got_2, got_3):
            total += got[:, columns].astype(F32)
        near[:, columns] = total[:rows]
        far[:, columns] = total[rows:].astype(BF16)


def sum_side_kernel(mine, got, *outs):
    rows = outs[0].shape[0] // 2
    for columns in tiles_of(mine.shape[1]):
        for distance, out in enumerate(outs):
            for core in range(2):
                start = (core * N_Y + distance) * rows
                block = slice(start, start + rows)
                total = mine[block, columns].astype(F32) + got[block, columns].astype(F32)
                out[core * rows : (core + 1) * rows, columns] = total.astype(out.dtype)


def gelu_kernel(offset, place, *refs):
    terms = refs[:-3]
    cot, act, grad = refs[-3:]
    rows = act.shape[0] // 2
    for side in range(2):
        core = lax.rem(place[2] + side, 2)
        block = slice(side * rows, (side + 1) * rows)
        absolute = pl.ds(pl.multiple_of(core * rows, rows), rows)
        for columns in tiles_of(act.shape[1]):
            pre = terms[0][block, columns].astype(F32)
            for term in terms[1:]:
                pre += term[block, columns].astype(F32)
            value, slope = gelu_parts(pre)
            act[absolute, columns] = value.astype(BF16)
            from_cot = slice(offset + columns.start, offset + columns.stop)
            grad[block, columns] = (cot[absolute, from_cot].astype(F32) * slope).astype(BF16)


def gelu_step(place, terms, cot, offset, name):
    shape = terms[0].shape
    size = shape[0] * shape[1]
    return call(
        functools.partial(gelu_kernel, offset),
        name,
        [(shape, BF16, ON_CHIP), (shape, BF16, ON_CHIP)],
        [SCALARS] + [ON_CHIP] * (len(terms) + 1),
        [place, *terms, cot],
        flops=40 * size,
        size=8 * size,
        transcendentals=size,
    )


def last_sum_kernel(got, out):
    for columns in tiles_of(out.shape[1]):
        total = got[0, :, columns].astype(F32)
        for i in range(1, got.shape[0]):
            total += got[i, :, columns].astype(F32)
        out[:, columns] = total.astype(BF16)


def local(tokens, weight, cotangent):
    rows, width = tokens.shape
    block, hidden = cotangent.shape
    cut = hidden // 2
    part_a, part_b = slice(0, cut), slice(cut, hidden)
    small_a, small_b = (block, cut), (block, hidden - cut)
    place = jnp.stack([lax.axis_index(a) for a in ("y", "xh", "c")]).astype(jnp.int32)

    spread = jnp.broadcast_to(tokens[None], (8, rows, width))
    own = lax.all_to_all(spread, PLANE, 0, 0, tiled=True)
    other = other_core(own)

    held = load(after(weight, own), part_b, "load_forward")
    toks, *sides = forward_side(place, own, other, held)
    got_side = across(sides[1])
    parts = forward_distance(toks, weight, part_a)
    got_a = [ahead(parts[d], d) for d in (1, 2, 3)]
    got_side = after(got_side, parts[0])
    kept, *sent = call(
        sum_side_kernel,
        "sum_b",
        [(small_b, F32 if d == 0 else BF16, ON_CHIP) for d in range(N_Y)],
        [ON_CHIP] * 2,
        [sides[0], got_side],
        flops=8 * block * hidden,
        size=16 * block * hidden,
    )
    got_b = [ahead(sent[d - 1], d) for d in (1, 2, 3)]
    got_a = after(got_a, sent[0])
    near, far = call(
        sum_distance_kernel,
        "sum_a",
        [(small_a, F32, ON_CHIP), (small_a, BF16, ON_CHIP)],
        [ON_CHIP] * 4,
        [parts[0], *got_a],
        flops=8 * block * hidden,
        size=16 * block * hidden,
    )
    got_far = across(far)

    act_b, grad_b = gelu_step(place, [kept, *got_b], cotangent, cut, "gelu_b")
    by_y = [grad_b] + [ahead(grad_b, -d) for d in (1, 2, 3)]
    by_y_far = [across(grad) for grad in by_y]
    got_far = after(got_far, grad_b)
    act_a, grad_a = gelu_step(place, [near, got_far], cotangent, 0, "gelu_a")
    both = jnp.concatenate([grad_a, across(grad_a)], axis=0)
    wide = [both] + [ahead(both, -d) for d in (1, 2, 3)]
    late, toks = after((weight, toks), both)
    held_a, held_b = load(late, part_a, "load_a"), load(late, part_b, "load_b")
    turned = turn(toks)
    activated = jnp.concatenate([act_a, act_b], axis=1)

    grads_b = [*by_y, *by_y_far]
    pieces_b = tuple(((d, s),) for s in range(2) for d in range(N_Y))
    begun = backward_first(after(grads_b, held_a, held_b, turned, activated), held_b, pieces_b)
    wide_last = after(wide, begun)
    theirs = backward_last(place, wide_last, held_a, begun, BY_DISTANCE, 1, "backward_other")
    arrived = other_core(theirs)
    wide_last = after(wide_last, theirs)
    mine = backward_last(place, wide_last, held_a, begun, BY_DISTANCE, 0, "backward_own")
    (chip,) = call(
        add_kernel,
        "chip_sum",
        [(mine.shape, BF16, ON_CHIP)],
        [ON_CHIP] * 2,
        [mine, arrived],
        flops=mine.size,
        size=6 * mine.size,
    )
    last = lax.all_to_all(chip, PLANE, 0, 0, tiled=True)
    grads = after([*grads_b, *wide], chip)
    offsets = [cut] * len(grads_b) + [0] * len(wide)
    weight_grad = weight_grad_of(turned, grads, pieces_b + BY_DISTANCE, offsets, hidden)
    (input_grad,) = call(
        last_sum_kernel,
        "last_sum",
        [((rows, width), BF16, ON_CHIP)],
        [ON_CHIP],
        [last],
        flops=8 * rows * width,
        size=16 * rows * width,
    )
    return (activated, input_grad, weight_grad)


def solution(mesh):
    fine = Mesh(mesh.devices.reshape(N_Y, 2, 2, 4, 2), ("y", "xh", "xl", "z", "c"))
    col = ("xl", "z", "c")
    return jax.shard_map(
        local,
        mesh=fine,
        in_specs=(P(col, ROW), P(ROW, col), P(ROW, col)),
        out_specs=(P(ROW, col), P(col, ROW), P(ROW, col)),
        check_vma=False,
    )
```

```python
import functools

import jax
import jax.numpy as jnp
from jax import lax
from jax.experimental import pallas as pl
from jax.experimental.pallas import tpu as pltpu
from jax.sharding import Mesh
from jax.sharding import PartitionSpec as P

N_Y = 4
ROW = ("y", "xh")
PLANE = ("xl", "z")
SWAP = ((0, 1), (1, 0))
MIB = 2**20
STEP = 512
F32, BF16 = jnp.float32, jnp.bfloat16
ON_CHIP = pl.BlockSpec(memory_space=pltpu.VMEM)
SCALARS = pl.BlockSpec(memory_space=pltpu.SMEM)
ANYWHERE = pl.BlockSpec(memory_space=pl.ANY)
IN_HBM = pl.BlockSpec(memory_space=pltpu.HBM)
BY_DISTANCE = tuple(((d, 0), (d, 1)) for d in range(N_Y))
BY_SIDE = tuple(tuple((d, s) for d in range(N_Y)) for s in range(2))


def gelu_parts(pre):
    coeff = 0.7978845608
    inner = coeff * (pre + 0.044715 * pre * pre * pre)
    tval = jnp.tanh(inner)
    value = 0.5 * pre * (1.0 + tval)
    slope = 0.5 * (1.0 + tval) + 0.5 * pre * (1.0 - tval * tval) * coeff * (
        1.0 + 3.0 * 0.044715 * pre * pre
    )
    return (value, slope)


def ahead(array, distance):
    return lax.ppermute(array, "y", [(i, (i + distance) % N_Y) for i in range(N_Y)])


def across(array):
    return lax.ppermute(array, "xh", SWAP)


def other_core(array):
    return lax.ppermute(array, "c", SWAP)


def after(value, *others):
    return lax.optimization_barrier((value, others))[0]


def block_of(place, distance, side):
    return lax.rem(place[0] + distance, N_Y) * 2 + lax.rem(place[1] + side, 2)


def tiles_of(width):
    return [slice(i, i + STEP) for i in range(0, width, STEP)]


def call(kernel, name, outs, ins, args, flops, size, transcendentals=0, scratch=(), limit=16, aliases=None):
    return pl.pallas_call(
        kernel,
        out_shape=[jax.ShapeDtypeStruct(shape, dtype) for shape, dtype, _ in outs],
        in_specs=ins,
        out_specs=[spec for _, _, spec in outs],
        scratch_shapes=list(scratch),
        input_output_aliases=aliases or {},
        compiler_params=pltpu.CompilerParams(vmem_limit_bytes=limit * MIB),
        cost_estimate=pl.CostEstimate(
            flops=flops, bytes_accessed=size, transcendentals=transcendentals
        ),
        name=name,
    )(*args)


def load_kernel(offset, source, out, sem):
    columns = slice(offset, offset + out.shape[1])
    copy = pltpu.make_async_copy(source.at[:, columns], out, sem)
    copy.start()
    copy.wait()


def load(weight, part, name):
    width = weight.shape[0]
    count = part.stop - part.start
    return call(
        functools.partial(load_kernel, part.start),
        name,
        [((width, count), BF16, ON_CHIP)],
        [ANYWHERE],
        [weight],
        flops=0,
        size=4 * width * count,
        scratch=[pltpu.SemaphoreType.DMA(())],
        limit=48,
    )[0]


def row_of(rows, core, distance, side):
    return (core * 2 * N_Y + 2 * distance + side) * rows


def place_tokens(place, tokens, held, core):
    rows = tokens.shape[1]
    for distance in range(N_Y):
        for side in range(2):
            start = row_of(rows, core, distance, side)
            held[start : start + rows, :] = tokens[block_of(place, distance, side)]


def put_sides(part, outs, columns, rows, core):
    for side, out in enumerate(outs):
        for distance in range(N_Y):
            start, to = (2 * distance + side) * rows, (core * N_Y + distance) * rows
            out[to : to + rows, columns] = part[start : start + rows, :]


def forward_side_kernel(place, own, other, weight, toks, first, second):
    rows = own.shape[1]
    place_tokens(place, own, toks, 0)
    place_tokens(place, other, toks, 1)

    def body(i, carry):
        columns = pl.ds(pl.multiple_of(i * STEP, STEP), STEP)
        part = jnp.dot(toks[...], weight[:, columns], preferred_element_type=F32).astype(BF16)
        for core in range(2):
            start = row_of(rows, core, 0, 0)
            put_sides(part[start : start + 2 * N_Y * rows], (first, second), columns, rows, core)
        return carry

    lax.fori_loop(0, weight.shape[1] // STEP, body, 0)


def forward_side(place, own, other, weight):
    blocks, rows, width = own.shape
    count = weight.shape[1]
    side = ((blocks * rows, count), BF16, ON_CHIP)
    return call(
        forward_side_kernel,
        "forward_side",
        [((2 * blocks * rows, width), BF16, ON_CHIP), side, side],
        [SCALARS] + [ON_CHIP] * 3,
        [place, own, other, weight],
        flops=4 * blocks * rows * width * count,
        size=2 * width * count,
    )


def forward_distance_kernel(part, toks, weight, *outs):
    rows = outs[0].shape[0] // 4

    def body(i, carry):
        columns = pl.ds(pl.multiple_of(i * STEP, STEP), STEP)
        taken = pl.ds(pl.multiple_of(part.start + i * STEP, STEP), STEP)
        sums = jnp.dot(toks[...], weight[:, taken], preferred_element_type=F32).astype(BF16)
        for distance, out in enumerate(outs):
            for side in range(2):
                for core in range(2):
                    start, to = row_of(rows, core, distance, side), (2 * side + core) * rows
                    out[to : to + rows, columns] = sums[start : start + rows, :]
        return carry

    lax.fori_loop(0, (part.stop - part.start) // STEP, body, 0)


def forward_distance(toks, weight, part):
    tokens, width = toks.shape
    count = part.stop - part.start
    return call(
        functools.partial(forward_distance_kernel, part),
        "forward_distance",
        [((tokens // N_Y, count), BF16, ON_CHIP)] * N_Y,
        [ON_CHIP, ON_CHIP],
        [toks, weight],
        flops=2 * tokens * width * count,
        size=2 * width * count,
    )


def assemble(grads, pieces, held, core):
    rows = held.shape[0] // (2 * N_Y)
    for grad, piece in zip(grads, pieces):
        for slot, (distance, side) in enumerate(piece):
            start, at = (2 * distance + side) * rows, (2 * slot + core) * rows
            held[start : start + rows, :] = grad[at : at + rows, :]


def times_weight(grad, weight, columns, part):
    return lax.dot_general(
        grad, weight[columns, part], (((1,), (1,)), ((), ())), preferred_element_type=F32
    )


def backward_first_kernel(pieces, part, *refs):
    grads = refs[: len(pieces)]
    weight, out, held = refs[len(pieces) :]
    half = held.shape[0] // 2
    for core in range(2):
        assemble(grads, pieces, held.at[core * half : (core + 1) * half], core)

    def body(i, carry):
        columns = pl.ds(pl.multiple_of(i * STEP, STEP), STEP)
        out[:, columns] = times_weight(held[...], weight, columns, part)
        return carry

    lax.fori_loop(0, weight.shape[0] // STEP, body, 0)


def backward_first(grads, weight, pieces, part):
    width, hidden = weight.shape[0], part.stop - part.start
    count = sum(grad.shape[0] for grad in grads)
    return call(
        functools.partial(backward_first_kernel, pieces, part),
        "backward_first",
        [((count, width), F32, ON_CHIP)],
        [ON_CHIP] * (len(grads) + 1),
        [*grads, weight],
        flops=2 * count * width * hidden,
        size=2 * width * hidden,
        scratch=[pltpu.VMEM((count, hidden), BF16)],
    )[0]


def backward_last_kernel(pieces, part, core, place, *refs):
    grads = refs[: len(pieces)]
    weight, begun, out, held = refs[len(pieces) :]
    assemble(grads, pieces, held, core)
    rows = out.shape[1]
    half = slice(core * 2 * N_Y * rows, (core + 1) * 2 * N_Y * rows)

    def body(i, carry):
        columns = pl.ds(pl.multiple_of(i * STEP, STEP), STEP)
        total = begun[half, columns] + times_weight(held[...], weight, columns, part)
        total = total.astype(BF16)
        for distance in range(N_Y):
            for side in range(2):
                start = (2 * distance + side) * rows
                out[block_of(place, distance, side), :, columns] = total[start : start + rows, :]
        return carry

    lax.fori_loop(0, weight.shape[0] // STEP, body, 0)


def backward_last(place, grads, weight, begun, pieces, part, core, name):
    width, hidden = weight.shape[0], part.stop - part.start
    count = begun.shape[0] // 2
    return call(
        functools.partial(backward_last_kernel, pieces, part, core),
        name,
        [((2 * N_Y, count // (2 * N_Y), width), BF16, ON_CHIP)],
        [SCALARS] + [ON_CHIP] * (len(grads) + 2),
        [place, *grads, weight, begun],
        flops=2 * count * width * hidden,
        size=2 * width * hidden,
        scratch=[pltpu.VMEM((count, hidden), BF16)],
    )[0]


def add_kernel(mine, got, out):
    for block in range(out.shape[0]):
        out[block] = (mine[block].astype(F32) + got[block].astype(F32)).astype(BF16)


def turn_kernel(tok, out, held, sem):
    held[...] = tok[...].T
    copy = pltpu.make_async_copy(held, out, sem)
    copy.start()
    copy.wait()


def turn(tok):
    rows, width = tok.shape
    return call(
        turn_kernel,
        "turn_tokens",
        [((width, rows), BF16, IN_HBM)],
        [ON_CHIP],
        [tok],
        flops=0,
        size=4 * rows * width,
        scratch=[pltpu.VMEM((width, rows), BF16), pltpu.SemaphoreType.DMA(())],
    )[0]


def weight_grad_kernel(pieces, offsets, *refs):
    turned, *grads = refs[: len(pieces) + 1]
    out, held_turned, held, tiles, sems, load_sems = refs[len(pieces) + 1 :]
    step = tiles.shape[2]
    steps = held.shape[1] // step
    rows = held.shape[0] // (4 * N_Y)
    loads = [pltpu.make_async_copy(turned, held_turned, load_sems.at[0])]
    for grad, piece, offset in zip(grads, pieces, offsets):
        columns = slice(offset, offset + grad.shape[1])
        for slot, (distance, side) in enumerate(piece):
            for core in range(2):
                start, at = row_of(rows, core, distance, side), (2 * slot + core) * rows
                loads.append(
                    pltpu.make_async_copy(
                        grad.at[at : at + rows, :],
                        held.at[start : start + rows, columns],
                        load_sems.at[len(loads)],
                    )
                )
    for load in loads:
        load.start()
    for load in loads:
        load.wait()

    def copy(i):
        columns = pl.ds(pl.multiple_of(i * step, step), step)
        slot = lax.rem(i, 2)
        return pltpu.make_async_copy(tiles.at[slot], out.at[:, columns], sems.at[slot])

    def body(i, carry):
        columns = pl.ds(pl.multiple_of(i * step, step), step)

        @pl.when(i >= 2)
        def _():
            copy(i - 2).wait()

        total = jnp.dot(held_turned[...], held[:, columns], preferred_element_type=F32)
        tiles[lax.rem(i, 2)] = total.astype(BF16)
        copy(i).start()
        return carry

    lax.fori_loop(0, steps, body, 0)
    copy(steps - 2).wait()
    copy(steps - 1).wait()


def weight_grad_of(turned, grads, pieces, offsets, hidden):
    width, rows = turned.shape
    return call(
        functools.partial(weight_grad_kernel, pieces, offsets),
        "weight_grad",
        [((width, hidden), BF16, IN_HBM)],
        [ANYWHERE] * (1 + len(grads)),
        [turned, *grads],
        flops=2 * rows * width * hidden,
        size=2 * width * hidden,
        scratch=[
            pltpu.VMEM(turned.shape, BF16),
            pltpu.VMEM((rows, hidden), BF16),
            pltpu.VMEM((2, width, STEP), BF16),
            pltpu.SemaphoreType.DMA((2,)),
            pltpu.SemaphoreType.DMA((1 + 2 * sum(len(piece) for piece in pieces),)),
        ],
        limit=56,
    )[0]


def sum_distance_kernel(mine, got_1, got_2, got_3, near, far):
    rows = near.shape[0]
    for columns in tiles_of(near.shape[1]):
        total = mine[:, columns].astype(F32)
        for got in (got_1, got_2, got_3):
            total += got[:, columns].astype(F32)
        near[:, columns] = total[:rows]
        far[:, columns] = total[rows:].astype(BF16)


def sum_side_kernel(mine, got, *outs):
    rows = outs[0].shape[0] // 2
    for columns in tiles_of(mine.shape[1]):
        for distance, out in enumerate(outs):
            for core in range(2):
                start = (core * N_Y + distance) * rows
                block = slice(start, start + rows)
                total = mine[block, columns].astype(F32) + got[block, columns].astype(F32)
                out[core * rows : (core + 1) * rows, columns] = total.astype(out.dtype)


def gelu_kernel(offset, place, *refs):
    terms = refs[:-3]
    cot, act, grad = refs[-3:]
    rows = act.shape[0] // 2
    for side in range(2):
        core = lax.rem(place[2] + side, 2)
        block = slice(side * rows, (side + 1) * rows)
        absolute = pl.ds(pl.multiple_of(core * rows, rows), rows)
        for columns in tiles_of(act.shape[1]):
            pre = terms[0][block, columns].astype(F32)
            for term in terms[1:]:
                pre += term[block, columns].astype(F32)
            value, slope = gelu_parts(pre)
            act[absolute, columns] = value.astype(BF16)
            from_cot = slice(offset + columns.start, offset + columns.stop)
            grad[block, columns] = (cot[absolute, from_cot].astype(F32) * slope).astype(BF16)


def gelu_step(place, terms, cot, offset, name):
    shape = terms[0].shape
    size = shape[0] * shape[1]
    return call(
        functools.partial(gelu_kernel, offset),
        name,
        [(shape, BF16, ON_CHIP), (shape, BF16, ON_CHIP)],
        [SCALARS] + [ON_CHIP] * (len(terms) + 1),
        [place, *terms, cot],
        flops=40 * size,
        size=8 * size,
        transcendentals=size,
    )


def last_sum_kernel(got, out):
    for columns in tiles_of(out.shape[1]):
        total = got[0, :, columns].astype(F32)
        for i in range(1, got.shape[0]):
            total += got[i, :, columns].astype(F32)
        out[:, columns] = total.astype(BF16)


def local(tokens, weight, cotangent):
    rows, width = tokens.shape
    block, hidden = cotangent.shape
    cut = hidden // 2
    part_a, part_b = slice(0, cut), slice(cut, hidden)
    small_a, small_b = (block, cut), (block, hidden - cut)
    place = jnp.stack([lax.axis_index(a) for a in ("y", "xh", "c")]).astype(jnp.int32)

    spread = jnp.broadcast_to(tokens[None], (8, rows, width))
    own = lax.all_to_all(spread, PLANE, 0, 0, tiled=True)
    other = other_core(own)

    held = load(after(weight, own), part_b, "load_forward")
    toks, *sides = forward_side(place, own, other, held)
    got_side = across(sides[1])
    parts = forward_distance(toks, weight, part_a)
    got_a = [ahead(parts[d], d) for d in (1, 2, 3)]
    got_side = after(got_side, parts[0])
    kept, *sent = call(
        sum_side_kernel,
        "sum_b",
        [(small_b, F32 if d == 0 else BF16, ON_CHIP) for d in range(N_Y)],
        [ON_CHIP] * 2,
        [sides[0], got_side],
        flops=8 * block * hidden,
        size=16 * block * hidden,
    )
    got_b = [ahead(sent[d - 1], d) for d in (1, 2, 3)]
    got_a = after(got_a, sent[0])
    near, far = call(
        sum_distance_kernel,
        "sum_a",
        [(small_a, F32, ON_CHIP), (small_a, BF16, ON_CHIP)],
        [ON_CHIP] * 4,
        [parts[0], *got_a],
        flops=8 * block * hidden,
        size=16 * block * hidden,
    )
    got_far = across(far)

    act_b, grad_b = gelu_step(place, [kept, *got_b], cotangent, cut, "gelu_b")
    by_y = [grad_b] + [ahead(grad_b, -d) for d in (1, 2, 3)]
    by_y_far = [across(grad) for grad in by_y]
    got_far = after(got_far, grad_b)
    act_a, grad_a = gelu_step(place, [near, got_far], cotangent, 0, "gelu_a")
    both = jnp.concatenate([grad_a, across(grad_a)], axis=0)
    wide = [both] + [ahead(both, -d) for d in (1, 2, 3)]
    turned = turn(after(toks, both))
    activated = jnp.concatenate([act_a, act_b], axis=1)

    grads_b = [*by_y, *by_y_far]
    pieces_b = tuple(((d, s),) for s in range(2) for d in range(N_Y))
    begun = backward_first(after(grads_b, turned, activated), weight, pieces_b, part_b)
    wide_last = after(wide, begun)
    theirs = backward_last(place, wide_last, weight, begun, BY_DISTANCE, part_a, 1, "backward_other")
    arrived = other_core(theirs)
    wide_last = after(wide_last, theirs)
    mine = backward_last(place, wide_last, weight, begun, BY_DISTANCE, part_a, 0, "backward_own")
    (chip,) = call(
        add_kernel,
        "chip_sum",
        [(mine.shape, BF16, ON_CHIP)],
        [ON_CHIP] * 2,
        [mine, arrived],
        flops=mine.size,
        size=6 * mine.size,
    )
    last = lax.all_to_all(chip, PLANE, 0, 0, tiled=True)
    grads = after([*grads_b, *wide], chip)
    offsets = [cut] * len(grads_b) + [0] * len(wide)
    weight_grad = weight_grad_of(turned, grads, pieces_b + BY_DISTANCE, offsets, hidden)
    (input_grad,) = call(
        last_sum_kernel,
        "last_sum",
        [((rows, width), BF16, ON_CHIP)],
        [ON_CHIP],
        [last],
        flops=8 * rows * width,
        size=16 * rows * width,
    )
    return (activated, input_grad, weight_grad)


def solution(mesh):
    fine = Mesh(mesh.devices.reshape(N_Y, 2, 2, 4, 2), ("y", "xh", "xl", "z", "c"))
    col = ("xl", "z", "c")
    return jax.shard_map(
        local,
        mesh=fine,
        in_specs=(P(col, ROW), P(ROW, col), P(ROW, col)),
        out_specs=(P(ROW, col), P(col, ROW), P(ROW, col)),
        check_vma=False,
    )
```

```python
import functools

import jax
import jax.numpy as jnp
from jax import lax
from jax.experimental import pallas as pl
from jax.experimental.pallas import tpu as pltpu
from jax.sharding import Mesh
from jax.sharding import PartitionSpec as P

N_Y = 4
ROW = ("y", "xh")
PLANE = ("xl", "z")
SWAP = ((0, 1), (1, 0))
MIB = 2**20
STEP = 512
F32, BF16 = jnp.float32, jnp.bfloat16
ON_CHIP = pl.BlockSpec(memory_space=pltpu.VMEM)
SCALARS = pl.BlockSpec(memory_space=pltpu.SMEM)
ANYWHERE = pl.BlockSpec(memory_space=pl.ANY)
IN_HBM = pl.BlockSpec(memory_space=pltpu.HBM)
BY_DISTANCE = tuple(((d, 0), (d, 1)) for d in range(N_Y))
BY_SIDE = tuple(tuple((d, s) for d in range(N_Y)) for s in range(2))


def gelu_parts(pre):
    coeff = 0.7978845608
    inner = coeff * (pre + 0.044715 * pre * pre * pre)
    tval = jnp.tanh(inner)
    value = 0.5 * pre * (1.0 + tval)
    slope = 0.5 * (1.0 + tval) + 0.5 * pre * (1.0 - tval * tval) * coeff * (
        1.0 + 3.0 * 0.044715 * pre * pre
    )
    return (value, slope)


def ahead(array, distance):
    return lax.ppermute(array, "y", [(i, (i + distance) % N_Y) for i in range(N_Y)])


def across(array):
    return lax.ppermute(array, "xh", SWAP)


def other_core(array):
    return lax.ppermute(array, "c", SWAP)


def after(value, *others):
    return lax.optimization_barrier((value, others))[0]


def block_of(place, distance, side):
    return lax.rem(place[0] + distance, N_Y) * 2 + lax.rem(place[1] + side, 2)


def tiles_of(width):
    return [slice(i, i + STEP) for i in range(0, width, STEP)]


def call(kernel, name, outs, ins, args, flops, size, transcendentals=0, scratch=(), limit=16, aliases=None):
    return pl.pallas_call(
        kernel,
        out_shape=[jax.ShapeDtypeStruct(shape, dtype) for shape, dtype, _ in outs],
        in_specs=ins,
        out_specs=[spec for _, _, spec in outs],
        scratch_shapes=list(scratch),
        input_output_aliases=aliases or {},
        compiler_params=pltpu.CompilerParams(vmem_limit_bytes=limit * MIB),
        cost_estimate=pl.CostEstimate(
            flops=flops, bytes_accessed=size, transcendentals=transcendentals
        ),
        name=name,
    )(*args)


def load_kernel(offset, source, out, sem):
    columns = slice(offset, offset + out.shape[1])
    copy = pltpu.make_async_copy(source.at[:, columns], out, sem)
    copy.start()
    copy.wait()


def load(weight, part, name):
    width = weight.shape[0]
    count = part.stop - part.start
    return call(
        functools.partial(load_kernel, part.start),
        name,
        [((width, count), BF16, ON_CHIP)],
        [ANYWHERE],
        [weight],
        flops=0,
        size=4 * width * count,
        scratch=[pltpu.SemaphoreType.DMA(())],
        limit=48,
    )[0]


def row_of(rows, core, distance, side):
    return (core * 2 * N_Y + 2 * distance + side) * rows


def place_tokens(place, tokens, held, core):
    rows = tokens.shape[1]
    for distance in range(N_Y):
        for side in range(2):
            start = row_of(rows, core, distance, side)
            held[start : start + rows, :] = tokens[block_of(place, distance, side)]


def put_sides(part, outs, columns, rows, core):
    for side, out in enumerate(outs):
        for distance in range(N_Y):
            start, to = (2 * distance + side) * rows, (core * N_Y + distance) * rows
            out[to : to + rows, columns] = part[start : start + rows, :]


def forward_side_kernel(place, own, other, weight, toks, first, second):
    rows = own.shape[1]
    place_tokens(place, own, toks, 0)
    place_tokens(place, other, toks, 1)

    def body(i, carry):
        columns = pl.ds(pl.multiple_of(i * STEP, STEP), STEP)
        part = jnp.dot(toks[...], weight[:, columns], preferred_element_type=F32).astype(BF16)
        for core in range(2):
            start = row_of(rows, core, 0, 0)
            put_sides(part[start : start + 2 * N_Y * rows], (first, second), columns, rows, core)
        return carry

    lax.fori_loop(0, weight.shape[1] // STEP, body, 0)


def forward_side(place, own, other, weight):
    blocks, rows, width = own.shape
    count = weight.shape[1]
    side = ((blocks * rows, count), BF16, ON_CHIP)
    return call(
        forward_side_kernel,
        "forward_side",
        [((2 * blocks * rows, width), BF16, ON_CHIP), side, side],
        [SCALARS] + [ON_CHIP] * 3,
        [place, own, other, weight],
        flops=4 * blocks * rows * width * count,
        size=2 * width * count,
    )


def forward_distance_kernel(part, toks, weight, *outs):
    rows = outs[0].shape[0] // 4

    def body(i, carry):
        columns = pl.ds(pl.multiple_of(i * STEP, STEP), STEP)
        taken = pl.ds(pl.multiple_of(part.start + i * STEP, STEP), STEP)
        sums = jnp.dot(toks[...], weight[:, taken], preferred_element_type=F32).astype(BF16)
        for distance, out in enumerate(outs):
            for side in range(2):
                for core in range(2):
                    start, to = row_of(rows, core, distance, side), (2 * side + core) * rows
                    out[to : to + rows, columns] = sums[start : start + rows, :]
        return carry

    lax.fori_loop(0, (part.stop - part.start) // STEP, body, 0)


def forward_distance(toks, weight, part):
    tokens, width = toks.shape
    count = part.stop - part.start
    return call(
        functools.partial(forward_distance_kernel, part),
        "forward_distance",
        [((tokens // N_Y, count), BF16, ON_CHIP)] * N_Y,
        [ON_CHIP, ON_CHIP],
        [toks, weight],
        flops=2 * tokens * width * count,
        size=2 * width * count,
    )


def assemble(grads, pieces, held, core):
    rows = held.shape[0] // (2 * N_Y)
    for grad, piece in zip(grads, pieces):
        for slot, (distance, side) in enumerate(piece):
            start, at = (2 * distance + side) * rows, (2 * slot + core) * rows
            held[start : start + rows, :] = grad[at : at + rows, :]


def times_weight(grad, weight, columns, part):
    return lax.dot_general(
        grad, weight[columns, part], (((1,), (1,)), ((), ())), preferred_element_type=F32
    )


def backward_first_kernel(pieces, part, *refs):
    grads = refs[: len(pieces)]
    weight, out, held = refs[len(pieces) :]
    half = held.shape[0] // 2
    for core in range(2):
        assemble(grads, pieces, held.at[core * half : (core + 1) * half], core)

    def body(i, carry):
        columns = pl.ds(pl.multiple_of(i * STEP, STEP), STEP)
        out[:, columns] = times_weight(held[...], weight, columns, part)
        return carry

    lax.fori_loop(0, weight.shape[0] // STEP, body, 0)


def backward_first(grads, weight, pieces, part):
    width, hidden = weight.shape[0], part.stop - part.start
    count = sum(grad.shape[0] for grad in grads)
    return call(
        functools.partial(backward_first_kernel, pieces, part),
        "backward_first",
        [((count, width), F32, ON_CHIP)],
        [ON_CHIP] * (len(grads) + 1),
        [*grads, weight],
        flops=2 * count * width * hidden,
        size=2 * width * hidden,
        scratch=[pltpu.VMEM((count, hidden), BF16)],
    )[0]


def backward_last_kernel(pieces, part, core, place, *refs):
    grads = refs[: len(pieces)]
    weight, begun, out, held = refs[len(pieces) :]
    assemble(grads, pieces, held, core)
    rows = out.shape[1]
    half = slice(core * 2 * N_Y * rows, (core + 1) * 2 * N_Y * rows)

    def body(i, carry):
        columns = pl.ds(pl.multiple_of(i * STEP, STEP), STEP)
        total = begun[half, columns] + times_weight(held[...], weight, columns, part)
        total = total.astype(BF16)
        for distance in range(N_Y):
            for side in range(2):
                start = (2 * distance + side) * rows
                out[block_of(place, distance, side), :, columns] = total[start : start + rows, :]
        return carry

    lax.fori_loop(0, weight.shape[0] // STEP, body, 0)


def backward_last(place, grads, weight, begun, pieces, part, core, name):
    width, hidden = weight.shape[0], part.stop - part.start
    count = begun.shape[0] // 2
    return call(
        functools.partial(backward_last_kernel, pieces, part, core),
        name,
        [((2 * N_Y, count // (2 * N_Y), width), BF16, ON_CHIP)],
        [SCALARS] + [ON_CHIP] * (len(grads) + 2),
        [place, *grads, weight, begun],
        flops=2 * count * width * hidden,
        size=2 * width * hidden,
        scratch=[pltpu.VMEM((count, hidden), BF16)],
    )[0]


def add_kernel(mine, got, out):
    out[...] = mine[...] + got[...]


def turn_kernel(tok, out, held, sem):
    held[...] = tok[...].T
    copy = pltpu.make_async_copy(held, out, sem)
    copy.start()
    copy.wait()


def turn(tok):
    rows, width = tok.shape
    return call(
        turn_kernel,
        "turn_tokens",
        [((width, rows), BF16, IN_HBM)],
        [ON_CHIP],
        [tok],
        flops=0,
        size=4 * rows * width,
        scratch=[pltpu.VMEM((width, rows), BF16), pltpu.SemaphoreType.DMA(())],
    )[0]


def weight_grad_kernel(pieces, offsets, *refs):
    turned, *grads = refs[: len(pieces) + 1]
    out, held_turned, held, tiles, sems, load_sems = refs[len(pieces) + 1 :]
    step = tiles.shape[2]
    steps = held.shape[1] // step
    rows = held.shape[0] // (4 * N_Y)
    loads = [pltpu.make_async_copy(turned, held_turned, load_sems.at[0])]
    for grad, piece, offset in zip(grads, pieces, offsets):
        columns = slice(offset, offset + grad.shape[1])
        for slot, (distance, side) in enumerate(piece):
            for core in range(2):
                start, at = row_of(rows, core, distance, side), (2 * slot + core) * rows
                loads.append(
                    pltpu.make_async_copy(
                        grad.at[at : at + rows, :],
                        held.at[start : start + rows, columns],
                        load_sems.at[len(loads)],
                    )
                )
    for load in loads:
        load.start()
    for load in loads:
        load.wait()

    def copy(i):
        columns = pl.ds(pl.multiple_of(i * step, step), step)
        slot = lax.rem(i, 2)
        return pltpu.make_async_copy(tiles.at[slot], out.at[:, columns], sems.at[slot])

    def body(i, carry):
        columns = pl.ds(pl.multiple_of(i * step, step), step)

        @pl.when(i >= 2)
        def _():
            copy(i - 2).wait()

        total = jnp.dot(held_turned[...], held[:, columns], preferred_element_type=F32)
        tiles[lax.rem(i, 2)] = total.astype(BF16)
        copy(i).start()
        return carry

    lax.fori_loop(0, steps, body, 0)
    copy(steps - 2).wait()
    copy(steps - 1).wait()


def weight_grad_of(turned, grads, pieces, offsets, hidden):
    width, rows = turned.shape
    return call(
        functools.partial(weight_grad_kernel, pieces, offsets),
        "weight_grad",
        [((width, hidden), BF16, IN_HBM)],
        [ANYWHERE] * (1 + len(grads)),
        [turned, *grads],
        flops=2 * rows * width * hidden,
        size=2 * width * hidden,
        scratch=[
            pltpu.VMEM(turned.shape, BF16),
            pltpu.VMEM((rows, hidden), BF16),
            pltpu.VMEM((2, width, STEP), BF16),
            pltpu.SemaphoreType.DMA((2,)),
            pltpu.SemaphoreType.DMA((1 + 2 * sum(len(piece) for piece in pieces),)),
        ],
        limit=56,
    )[0]


def sum_distance_kernel(mine, got_1, got_2, got_3, near, far):
    rows = near.shape[0]
    for columns in tiles_of(near.shape[1]):
        total = mine[:, columns].astype(F32)
        for got in (got_1, got_2, got_3):
            total += got[:, columns].astype(F32)
        near[:, columns] = total[:rows]
        far[:, columns] = total[rows:].astype(BF16)


def sum_side_kernel(mine, got, *outs):
    rows = outs[0].shape[0] // 2
    for columns in tiles_of(mine.shape[1]):
        for distance, out in enumerate(outs):
            for core in range(2):
                start = (core * N_Y + distance) * rows
                block = slice(start, start + rows)
                total = mine[block, columns].astype(F32) + got[block, columns].astype(F32)
                out[core * rows : (core + 1) * rows, columns] = total.astype(out.dtype)


def gelu_kernel(offset, place, *refs):
    terms = refs[:-3]
    cot, act, grad = refs[-3:]
    rows = act.shape[0] // 2
    for side in range(2):
        core = lax.rem(place[2] + side, 2)
        block = slice(side * rows, (side + 1) * rows)
        absolute = pl.ds(pl.multiple_of(core * rows, rows), rows)
        for columns in tiles_of(act.shape[1]):
            pre = terms[0][block, columns].astype(F32)
            for term in terms[1:]:
                pre += term[block, columns].astype(F32)
            value, slope = gelu_parts(pre)
            act[absolute, columns] = value.astype(BF16)
            from_cot = slice(offset + columns.start, offset + columns.stop)
            grad[block, columns] = (cot[absolute, from_cot].astype(F32) * slope).astype(BF16)


def gelu_step(place, terms, cot, offset, name):
    shape = terms[0].shape
    size = shape[0] * shape[1]
    return call(
        functools.partial(gelu_kernel, offset),
        name,
        [(shape, BF16, ON_CHIP), (shape, BF16, ON_CHIP)],
        [SCALARS] + [ON_CHIP] * (len(terms) + 1),
        [place, *terms, cot],
        flops=40 * size,
        size=8 * size,
        transcendentals=size,
    )


def last_sum_kernel(got, out):
    for columns in tiles_of(out.shape[1]):
        total = got[0, :, columns].astype(F32)
        for i in range(1, got.shape[0]):
            total += got[i, :, columns].astype(F32)
        out[:, columns] = total.astype(BF16)


def local(tokens, weight, cotangent):
    rows, width = tokens.shape
    block, hidden = cotangent.shape
    cut = hidden // 2
    part_a, part_b = slice(0, cut), slice(cut, hidden)
    small_a, small_b = (block, cut), (block, hidden - cut)
    place = jnp.stack([lax.axis_index(a) for a in ("y", "xh", "c")]).astype(jnp.int32)

    spread = jnp.broadcast_to(tokens[None], (8, rows, width))
    own = lax.all_to_all(spread, PLANE, 0, 0, tiled=True)
    other = other_core(own)

    held = load(after(weight, own), part_b, "load_forward")
    toks, *sides = forward_side(place, own, other, held)
    got_side = across(sides[1])
    parts = forward_distance(toks, weight, part_a)
    got_a = [ahead(parts[d], d) for d in (1, 2, 3)]
    got_side = after(got_side, parts[0])
    kept, *sent = call(
        sum_side_kernel,
        "sum_b",
        [(small_b, F32 if d == 0 else BF16, ON_CHIP) for d in range(N_Y)],
        [ON_CHIP] * 2,
        [sides[0], got_side],
        flops=8 * block * hidden,
        size=16 * block * hidden,
    )
    got_b = [ahead(sent[d - 1], d) for d in (1, 2, 3)]
    got_a = after(got_a, sent[0])
    near, far = call(
        sum_distance_kernel,
        "sum_a",
        [(small_a, F32, ON_CHIP), (small_a, BF16, ON_CHIP)],
        [ON_CHIP] * 4,
        [parts[0], *got_a],
        flops=8 * block * hidden,
        size=16 * block * hidden,
    )
    got_far = across(far)

    act_b, grad_b = gelu_step(place, [kept, *got_b], cotangent, cut, "gelu_b")
    got_far = after(got_far, grad_b)
    act_a, grad_a = gelu_step(place, [near, got_far], cotangent, 0, "gelu_a")
    late_b = after(grad_b, grad_a)
    by_y = [grad_b]
    by_y += [ahead(late_b if d == 1 else grad_b, -d) for d in (1, 2, 3)]
    by_y_far = [across(grad) for grad in by_y]
    both = jnp.concatenate([grad_a, across(grad_a)], axis=0)
    wide = [both] + [ahead(both, -d) for d in (1, 2, 3)]
    turned = turn(after(toks, both))
    activated = jnp.concatenate([act_a, act_b], axis=1)

    grads_b = [*by_y, *by_y_far]
    pieces_b = tuple(((d, s),) for s in range(2) for d in range(N_Y))
    begun = backward_first(after(grads_b, turned, activated), weight, pieces_b, part_b)
    wide_last = after(wide, begun)
    theirs = backward_last(place, wide_last, weight, begun, BY_DISTANCE, part_a, 1, "backward_other")
    arrived = other_core(theirs)
    wide_last = after(wide_last, theirs)
    mine = backward_last(place, wide_last, weight, begun, BY_DISTANCE, part_a, 0, "backward_own")
    (chip,) = call(
        add_kernel,
        "chip_sum",
        [(mine.shape, BF16, ON_CHIP)],
        [ON_CHIP] * 2,
        [mine, arrived],
        flops=mine.size,
        size=6 * mine.size,
    )
    last = lax.all_to_all(chip, PLANE, 0, 0, tiled=True)
    grads = after([*grads_b, *wide], chip)
    offsets = [cut] * len(grads_b) + [0] * len(wide)
    weight_grad = weight_grad_of(turned, grads, pieces_b + BY_DISTANCE, offsets, hidden)
    (input_grad,) = call(
        last_sum_kernel,
        "last_sum",
        [((rows, width), BF16, ON_CHIP)],
        [ON_CHIP],
        [last],
        flops=8 * rows * width,
        size=16 * rows * width,
    )
    return (activated, input_grad, weight_grad)


def solution(mesh):
    fine = Mesh(mesh.devices.reshape(N_Y, 2, 2, 4, 2), ("y", "xh", "xl", "z", "c"))
    col = ("xl", "z", "c")
    return jax.shard_map(
        local,
        mesh=fine,
        in_specs=(P(col, ROW), P(ROW, col), P(ROW, col)),
        out_specs=(P(ROW, col), P(col, ROW), P(ROW, col)),
        check_vma=False,
    )
```

```python
import functools

import jax
import jax.numpy as jnp
from jax import lax
from jax.experimental import pallas as pl
from jax.experimental.pallas import tpu as pltpu
from jax.sharding import Mesh
from jax.sharding import PartitionSpec as P

N_Y = 4
ROW = ("y", "xh")
PLANE = ("xl", "z")
SWAP = ((0, 1), (1, 0))
MIB = 2**20
STEP = 512
F32, BF16 = jnp.float32, jnp.bfloat16
ON_CHIP = pl.BlockSpec(memory_space=pltpu.VMEM)
SCALARS = pl.BlockSpec(memory_space=pltpu.SMEM)
ANYWHERE = pl.BlockSpec(memory_space=pl.ANY)
IN_HBM = pl.BlockSpec(memory_space=pltpu.HBM)
BY_DISTANCE = tuple(((d, 0), (d, 1)) for d in range(N_Y))
BY_SIDE = tuple(tuple((d, s) for d in range(N_Y)) for s in range(2))


def gelu_parts(pre):
    coeff = 0.7978845608
    inner = coeff * (pre + 0.044715 * pre * pre * pre)
    tval = jnp.tanh(inner)
    value = 0.5 * pre * (1.0 + tval)
    slope = 0.5 * (1.0 + tval) + 0.5 * pre * (1.0 - tval * tval) * coeff * (
        1.0 + 3.0 * 0.044715 * pre * pre
    )
    return (value, slope)


def ahead(array, distance):
    return lax.ppermute(array, "y", [(i, (i + distance) % N_Y) for i in range(N_Y)])


def across(array):
    return lax.ppermute(array, "xh", SWAP)


def other_core(array):
    return lax.ppermute(array, "c", SWAP)


def after(value, *others):
    return lax.optimization_barrier((value, others))[0]


def block_of(place, distance, side):
    return lax.rem(place[0] + distance, N_Y) * 2 + lax.rem(place[1] + side, 2)


def tiles_of(width):
    return [slice(i, i + STEP) for i in range(0, width, STEP)]


def call(kernel, name, outs, ins, args, flops, size, transcendentals=0, scratch=(), limit=16, aliases=None):
    return pl.pallas_call(
        kernel,
        out_shape=[jax.ShapeDtypeStruct(shape, dtype) for shape, dtype, _ in outs],
        in_specs=ins,
        out_specs=[spec for _, _, spec in outs],
        scratch_shapes=list(scratch),
        input_output_aliases=aliases or {},
        compiler_params=pltpu.CompilerParams(vmem_limit_bytes=limit * MIB),
        cost_estimate=pl.CostEstimate(
            flops=flops, bytes_accessed=size, transcendentals=transcendentals
        ),
        name=name,
    )(*args)


def load_kernel(offset, source, out, sem):
    columns = slice(offset, offset + out.shape[1])
    copy = pltpu.make_async_copy(source.at[:, columns], out, sem)
    copy.start()
    copy.wait()


def load(weight, part, name):
    width = weight.shape[0]
    count = part.stop - part.start
    return call(
        functools.partial(load_kernel, part.start),
        name,
        [((width, count), BF16, ON_CHIP)],
        [ANYWHERE],
        [weight],
        flops=0,
        size=4 * width * count,
        scratch=[pltpu.SemaphoreType.DMA(())],
        limit=48,
    )[0]


def row_of(rows, core, distance, side):
    return (core * 2 * N_Y + 2 * distance + side) * rows


def place_tokens(place, tokens, held, core):
    rows = tokens.shape[1]
    for distance in range(N_Y):
        for side in range(2):
            start = row_of(rows, core, distance, side)
            held[start : start + rows, :] = tokens[block_of(place, distance, side)]


def put_sides(part, outs, columns, rows, core):
    for side, out in enumerate(outs):
        for distance in range(N_Y):
            start, to = (2 * distance + side) * rows, (core * N_Y + distance) * rows
            out[to : to + rows, columns] = part[start : start + rows, :]


def forward_side_kernel(place, own, other, weight, toks, first, second):
    rows = own.shape[1]
    place_tokens(place, own, toks, 0)
    place_tokens(place, other, toks, 1)

    def body(i, carry):
        columns = pl.ds(pl.multiple_of(i * STEP, STEP), STEP)
        part = jnp.dot(toks[...], weight[:, columns], preferred_element_type=F32).astype(BF16)
        for core in range(2):
            start = row_of(rows, core, 0, 0)
            put_sides(part[start : start + 2 * N_Y * rows], (first, second), columns, rows, core)
        return carry

    lax.fori_loop(0, weight.shape[1] // STEP, body, 0)


def forward_side(place, own, other, weight):
    blocks, rows, width = own.shape
    count = weight.shape[1]
    side = ((blocks * rows, count), BF16, ON_CHIP)
    return call(
        forward_side_kernel,
        "forward_side",
        [((2 * blocks * rows, width), BF16, ON_CHIP), side, side],
        [SCALARS] + [ON_CHIP] * 3,
        [place, own, other, weight],
        flops=4 * blocks * rows * width * count,
        size=2 * width * count,
    )


def forward_distance_kernel(part, toks, weight, *outs):
    rows = outs[0].shape[0] // 4

    def body(i, carry):
        columns = pl.ds(pl.multiple_of(i * STEP, STEP), STEP)
        taken = pl.ds(pl.multiple_of(part.start + i * STEP, STEP), STEP)
        sums = jnp.dot(toks[...], weight[:, taken], preferred_element_type=F32).astype(BF16)
        for distance, out in enumerate(outs):
            for side in range(2):
                for core in range(2):
                    start, to = row_of(rows, core, distance, side), (2 * side + core) * rows
                    out[to : to + rows, columns] = sums[start : start + rows, :]
        return carry

    lax.fori_loop(0, (part.stop - part.start) // STEP, body, 0)


def forward_distance(toks, weight, part):
    tokens, width = toks.shape
    count = part.stop - part.start
    return call(
        functools.partial(forward_distance_kernel, part),
        "forward_distance",
        [((tokens // N_Y, count), BF16, ON_CHIP)] * N_Y,
        [ON_CHIP, ON_CHIP],
        [toks, weight],
        flops=2 * tokens * width * count,
        size=2 * width * count,
    )


def assemble(grads, pieces, held, core):
    rows = held.shape[0] // (2 * N_Y)
    for grad, piece in zip(grads, pieces):
        for slot, (distance, side) in enumerate(piece):
            start, at = (2 * distance + side) * rows, (2 * slot + core) * rows
            held[start : start + rows, :] = grad[at : at + rows, :]


def times_weight(grad, weight, columns, part):
    return lax.dot_general(
        grad, weight[columns, part], (((1,), (1,)), ((), ())), preferred_element_type=F32
    )


def backward_first_kernel(pieces, part, *refs):
    grads = refs[: len(pieces)]
    weight, out, held = refs[len(pieces) :]
    half = held.shape[0] // 2
    for core in range(2):
        assemble(grads, pieces, held.at[core * half : (core + 1) * half], core)

    def body(i, carry):
        columns = pl.ds(pl.multiple_of(i * STEP, STEP), STEP)
        out[:, columns] = times_weight(held[...], weight, columns, part)
        return carry

    lax.fori_loop(0, weight.shape[0] // STEP, body, 0)


def backward_first(grads, weight, pieces, part):
    width, hidden = weight.shape[0], part.stop - part.start
    count = sum(grad.shape[0] for grad in grads)
    return call(
        functools.partial(backward_first_kernel, pieces, part),
        "backward_first",
        [((count, width), F32, ON_CHIP)],
        [ON_CHIP] * (len(grads) + 1),
        [*grads, weight],
        flops=2 * count * width * hidden,
        size=2 * width * hidden,
        scratch=[pltpu.VMEM((count, hidden), BF16)],
    )[0]


def backward_last_kernel(pieces, part, core, place, *refs):
    grads = refs[: len(pieces)]
    weight, begun, out, held = refs[len(pieces) :]
    assemble(grads, pieces, held, core)
    rows = out.shape[1]
    half = slice(core * 2 * N_Y * rows, (core + 1) * 2 * N_Y * rows)

    def body(i, carry):
        columns = pl.ds(pl.multiple_of(i * STEP, STEP), STEP)
        total = begun[half, columns] + times_weight(held[...], weight, columns, part)
        total = total.astype(BF16)
        for distance in range(N_Y):
            for side in range(2):
                start = (2 * distance + side) * rows
                out[block_of(place, distance, side), :, columns] = total[start : start + rows, :]
        return carry

    lax.fori_loop(0, weight.shape[0] // STEP, body, 0)


def backward_last(place, grads, weight, begun, pieces, part, core, name):
    width, hidden = weight.shape[0], part.stop - part.start
    count = begun.shape[0] // 2
    return call(
        functools.partial(backward_last_kernel, pieces, part, core),
        name,
        [((2 * N_Y, count // (2 * N_Y), width), BF16, ON_CHIP)],
        [SCALARS] + [ON_CHIP] * (len(grads) + 2),
        [place, *grads, weight, begun],
        flops=2 * count * width * hidden,
        size=2 * width * hidden,
        scratch=[pltpu.VMEM((count, hidden), BF16)],
    )[0]


def add_kernel(mine, got, out):
    out[...] = mine[...] + got[...]


def turn_kernel(tok, out, held, sem):
    held[...] = tok[...].T
    copy = pltpu.make_async_copy(held, out, sem)
    copy.start()
    copy.wait()


def turn(tok):
    rows, width = tok.shape
    return call(
        turn_kernel,
        "turn_tokens",
        [((width, rows), BF16, IN_HBM)],
        [ON_CHIP],
        [tok],
        flops=0,
        size=4 * rows * width,
        scratch=[pltpu.VMEM((width, rows), BF16), pltpu.SemaphoreType.DMA(())],
    )[0]


def weight_grad_kernel(pieces, offsets, *refs):
    turned, *grads = refs[: len(pieces) + 1]
    out, held_turned, held, tiles, sems, load_sems = refs[len(pieces) + 1 :]
    step = tiles.shape[2]
    steps = held.shape[1] // step
    rows = held.shape[0] // (4 * N_Y)
    loads = [pltpu.make_async_copy(turned, held_turned, load_sems.at[0])]
    for grad, piece, offset in zip(grads, pieces, offsets):
        columns = slice(offset, offset + grad.shape[1])
        for slot, (distance, side) in enumerate(piece):
            for core in range(2):
                start, at = row_of(rows, core, distance, side), (2 * slot + core) * rows
                loads.append(
                    pltpu.make_async_copy(
                        grad.at[at : at + rows, :],
                        held.at[start : start + rows, columns],
                        load_sems.at[len(loads)],
                    )
                )
    for load in loads:
        load.start()
    for load in loads:
        load.wait()

    def copy(i):
        columns = pl.ds(pl.multiple_of(i * step, step), step)
        slot = lax.rem(i, 2)
        return pltpu.make_async_copy(tiles.at[slot], out.at[:, columns], sems.at[slot])

    def body(i, carry):
        columns = pl.ds(pl.multiple_of(i * step, step), step)

        @pl.when(i >= 2)
        def _():
            copy(i - 2).wait()

        total = jnp.dot(held_turned[...], held[:, columns], preferred_element_type=F32)
        tiles[lax.rem(i, 2)] = total.astype(BF16)
        copy(i).start()
        return carry

    lax.fori_loop(0, steps, body, 0)
    copy(steps - 2).wait()
    copy(steps - 1).wait()


def weight_grad_of(turned, grads, pieces, offsets, hidden):
    width, rows = turned.shape
    return call(
        functools.partial(weight_grad_kernel, pieces, offsets),
        "weight_grad",
        [((width, hidden), BF16, IN_HBM)],
        [ANYWHERE] * (1 + len(grads)),
        [turned, *grads],
        flops=2 * rows * width * hidden,
        size=2 * width * hidden,
        scratch=[
            pltpu.VMEM(turned.shape, BF16),
            pltpu.VMEM((rows, hidden), BF16),
            pltpu.VMEM((2, width, STEP), BF16),
            pltpu.SemaphoreType.DMA((2,)),
            pltpu.SemaphoreType.DMA((1 + 2 * sum(len(piece) for piece in pieces),)),
        ],
        limit=56,
    )[0]


def sum_distance_kernel(mine, got_1, got_2, got_3, near, far):
    rows = near.shape[0]
    for columns in tiles_of(near.shape[1]):
        total = mine[:, columns].astype(F32)
        for got in (got_1, got_2, got_3):
            total += got[:, columns].astype(F32)
        near[:, columns] = total[:rows]
        far[:, columns] = total[rows:].astype(BF16)


def sum_side_kernel(mine, got, *outs):
    rows = outs[0].shape[0] // 2
    for columns in tiles_of(mine.shape[1]):
        for distance, out in enumerate(outs):
            for core in range(2):
                start = (core * N_Y + distance) * rows
                block = slice(start, start + rows)
                total = mine[block, columns].astype(F32) + got[block, columns].astype(F32)
                out[core * rows : (core + 1) * rows, columns] = total.astype(out.dtype)


def gelu_kernel(offset, place, *refs):
    terms = refs[:-3]
    cot, act, grad = refs[-3:]
    rows = act.shape[0] // 2
    for side in range(2):
        core = lax.rem(place[2] + side, 2)
        block = slice(side * rows, (side + 1) * rows)
        absolute = pl.ds(pl.multiple_of(core * rows, rows), rows)
        for columns in tiles_of(act.shape[1]):
            pre = terms[0][block, columns].astype(F32)
            for term in terms[1:]:
                pre += term[block, columns].astype(F32)
            value, slope = gelu_parts(pre)
            act[absolute, columns] = value.astype(BF16)
            from_cot = slice(offset + columns.start, offset + columns.stop)
            grad[block, columns] = (cot[absolute, from_cot].astype(F32) * slope).astype(BF16)


def gelu_step(place, terms, cot, offset, name):
    shape = terms[0].shape
    size = shape[0] * shape[1]
    return call(
        functools.partial(gelu_kernel, offset),
        name,
        [(shape, BF16, ON_CHIP), (shape, BF16, ON_CHIP)],
        [SCALARS] + [ON_CHIP] * (len(terms) + 1),
        [place, *terms, cot],
        flops=40 * size,
        size=8 * size,
        transcendentals=size,
    )


def last_sum_kernel(got, out):
    for columns in tiles_of(out.shape[1]):
        total = got[0, :, columns].astype(F32)
        for i in range(1, got.shape[0]):
            total += got[i, :, columns].astype(F32)
        out[:, columns] = total.astype(BF16)


def local(tokens, weight, cotangent):
    rows, width = tokens.shape
    block, hidden = cotangent.shape
    cut = hidden // 2
    part_a, part_b = slice(0, cut), slice(cut, hidden)
    small_a, small_b = (block, cut), (block, hidden - cut)
    place = jnp.stack([lax.axis_index(a) for a in ("y", "xh", "c")]).astype(jnp.int32)

    spread = jnp.broadcast_to(tokens[None], (8, rows, width))
    own = lax.all_to_all(spread, PLANE, 0, 0, tiled=True)
    other = other_core(own)

    held = load(after(weight, own), part_b, "load_forward")
    toks, *sides = forward_side(place, own, other, held)
    got_side = across(sides[1])
    parts = forward_distance(toks, weight, part_a)
    got_a = [ahead(parts[d], d) for d in (1, 2, 3)]
    got_side = after(got_side, parts[0])
    kept, *sent = call(
        sum_side_kernel,
        "sum_b",
        [(small_b, F32 if d == 0 else BF16, ON_CHIP) for d in range(N_Y)],
        [ON_CHIP] * 2,
        [sides[0], got_side],
        flops=8 * block * hidden,
        size=16 * block * hidden,
    )
    got_b = [ahead(sent[d - 1], d) for d in (1, 2, 3)]
    got_a = after(got_a, sent[0])
    near, far = call(
        sum_distance_kernel,
        "sum_a",
        [(small_a, F32, ON_CHIP), (small_a, BF16, ON_CHIP)],
        [ON_CHIP] * 4,
        [parts[0], *got_a],
        flops=8 * block * hidden,
        size=16 * block * hidden,
    )
    got_far = across(far)

    act_b, grad_b = gelu_step(place, [kept, *got_b], cotangent, cut, "gelu_b")
    got_far = after(got_far, grad_b)
    act_a, grad_a = gelu_step(place, [near, got_far], cotangent, 0, "gelu_a")
    late_b = after(grad_b, grad_a)
    by_y = [grad_b]
    by_y += [ahead(late_b if d == 1 else grad_b, -d) for d in (1, 2, 3)]
    by_y_far = [across(grad) for grad in by_y]
    both = jnp.concatenate([grad_a, across(grad_a)], axis=0)
    wide = [both] + [ahead(after(both, by_y[2]) if d == 2 else both, -d) for d in (1, 2, 3)]
    turned = turn(after(toks, both))
    activated = jnp.concatenate([act_a, act_b], axis=1)

    grads_b = [*by_y, *by_y_far]
    pieces_b = tuple(((d, s),) for s in range(2) for d in range(N_Y))
    begun = backward_first(after(grads_b, turned, activated), weight, pieces_b, part_b)
    wide_last = after(wide, begun)
    theirs = backward_last(place, wide_last, weight, begun, BY_DISTANCE, part_a, 1, "backward_other")
    arrived = other_core(theirs)
    wide_last = after(wide_last, theirs)
    mine = backward_last(place, wide_last, weight, begun, BY_DISTANCE, part_a, 0, "backward_own")
    (chip,) = call(
        add_kernel,
        "chip_sum",
        [(mine.shape, BF16, ON_CHIP)],
        [ON_CHIP] * 2,
        [mine, arrived],
        flops=mine.size,
        size=6 * mine.size,
    )
    last = lax.all_to_all(chip, PLANE, 0, 0, tiled=True)
    grads = after([*grads_b, *wide], chip)
    offsets = [cut] * len(grads_b) + [0] * len(wide)
    weight_grad = weight_grad_of(turned, grads, pieces_b + BY_DISTANCE, offsets, hidden)
    (input_grad,) = call(
        last_sum_kernel,
        "last_sum",
        [((rows, width), BF16, ON_CHIP)],
        [ON_CHIP],
        [last],
        flops=8 * rows * width,
        size=16 * rows * width,
    )
    return (activated, input_grad, weight_grad)


def solution(mesh):
    fine = Mesh(mesh.devices.reshape(N_Y, 2, 2, 4, 2), ("y", "xh", "xl", "z", "c"))
    col = ("xl", "z", "c")
    return jax.shard_map(
        local,
        mesh=fine,
        in_specs=(P(col, ROW), P(ROW, col), P(ROW, col)),
        out_specs=(P(ROW, col), P(col, ROW), P(ROW, col)),
        check_vma=False,
    )
```

```python
import functools

import jax
import jax.numpy as jnp
from jax import lax
from jax.experimental import pallas as pl
from jax.experimental.pallas import tpu as pltpu
from jax.sharding import Mesh
from jax.sharding import PartitionSpec as P

N_Y = 4
ROW = ("y", "xh")
PLANE = ("xl", "z")
SWAP = ((0, 1), (1, 0))
MIB = 2**20
STEP = 512
F32, BF16 = jnp.float32, jnp.bfloat16
ON_CHIP = pl.BlockSpec(memory_space=pltpu.VMEM)
SCALARS = pl.BlockSpec(memory_space=pltpu.SMEM)
ANYWHERE = pl.BlockSpec(memory_space=pl.ANY)
IN_HBM = pl.BlockSpec(memory_space=pltpu.HBM)
BY_DISTANCE = tuple(((d, 0), (d, 1)) for d in range(N_Y))
BY_SIDE = tuple(tuple((d, s) for d in range(N_Y)) for s in range(2))


def gelu_parts(pre):
    coeff = 0.7978845608
    inner = coeff * (pre + 0.044715 * pre * pre * pre)
    tval = jnp.tanh(inner)
    value = 0.5 * pre * (1.0 + tval)
    slope = 0.5 * (1.0 + tval) + 0.5 * pre * (1.0 - tval * tval) * coeff * (
        1.0 + 3.0 * 0.044715 * pre * pre
    )
    return (value, slope)


def ahead(array, distance):
    return lax.ppermute(array, "y", [(i, (i + distance) % N_Y) for i in range(N_Y)])


def across(array):
    return lax.ppermute(array, "xh", SWAP)


def other_core(array):
    return lax.ppermute(array, "c", SWAP)


def after(value, *others):
    return lax.optimization_barrier((value, others))[0]


def block_of(place, distance, side):
    return lax.rem(place[0] + distance, N_Y) * 2 + lax.rem(place[1] + side, 2)


def tiles_of(width):
    return [slice(i, i + STEP) for i in range(0, width, STEP)]


def call(kernel, name, outs, ins, args, flops, size, transcendentals=0, scratch=(), limit=16, aliases=None):
    return pl.pallas_call(
        kernel,
        out_shape=[jax.ShapeDtypeStruct(shape, dtype) for shape, dtype, _ in outs],
        in_specs=ins,
        out_specs=[spec for _, _, spec in outs],
        scratch_shapes=list(scratch),
        input_output_aliases=aliases or {},
        compiler_params=pltpu.CompilerParams(vmem_limit_bytes=limit * MIB),
        cost_estimate=pl.CostEstimate(
            flops=flops, bytes_accessed=size, transcendentals=transcendentals
        ),
        name=name,
    )(*args)


def load_kernel(offset, source, out, sem):
    columns = slice(offset, offset + out.shape[1])
    copy = pltpu.make_async_copy(source.at[:, columns], out, sem)
    copy.start()
    copy.wait()


def load(weight, part, name):
    width = weight.shape[0]
    count = part.stop - part.start
    return call(
        functools.partial(load_kernel, part.start),
        name,
        [((width, count), BF16, ON_CHIP)],
        [ANYWHERE],
        [weight],
        flops=0,
        size=4 * width * count,
        scratch=[pltpu.SemaphoreType.DMA(())],
        limit=48,
    )[0]


def row_of(rows, core, distance, side):
    return (core * 2 * N_Y + 2 * distance + side) * rows


def place_tokens(place, tokens, held, core):
    rows = tokens.shape[1]
    for distance in range(N_Y):
        for side in range(2):
            start = row_of(rows, core, distance, side)
            held[start : start + rows, :] = tokens[block_of(place, distance, side)]


def put_sides(part, outs, columns, rows, core):
    for side, out in enumerate(outs):
        for distance in range(N_Y):
            start, to = (2 * distance + side) * rows, (core * N_Y + distance) * rows
            out[to : to + rows, columns] = part[start : start + rows, :]


def forward_side_kernel(place, own, other, weight, toks, first, second):
    rows = own.shape[1]
    place_tokens(place, own, toks, 0)
    place_tokens(place, other, toks, 1)

    def body(i, carry):
        columns = pl.ds(pl.multiple_of(i * STEP, STEP), STEP)
        part = jnp.dot(toks[...], weight[:, columns], preferred_element_type=F32).astype(BF16)
        for core in range(2):
            start = row_of(rows, core, 0, 0)
            put_sides(part[start : start + 2 * N_Y * rows], (first, second), columns, rows, core)
        return carry

    lax.fori_loop(0, weight.shape[1] // STEP, body, 0)


def forward_side(place, own, other, weight):
    blocks, rows, width = own.shape
    count = weight.shape[1]
    side = ((blocks * rows, count), BF16, ON_CHIP)
    return call(
        forward_side_kernel,
        "forward_side",
        [((2 * blocks * rows, width), BF16, ON_CHIP), side, side],
        [SCALARS] + [ON_CHIP] * 3,
        [place, own, other, weight],
        flops=4 * blocks * rows * width * count,
        size=2 * width * count,
    )


def forward_distance_kernel(part, toks, weight, *outs):
    rows = outs[0].shape[0] // 4

    def body(i, carry):
        columns = pl.ds(pl.multiple_of(i * STEP, STEP), STEP)
        taken = pl.ds(pl.multiple_of(part.start + i * STEP, STEP), STEP)
        sums = jnp.dot(toks[...], weight[:, taken], preferred_element_type=F32).astype(BF16)
        for distance, out in enumerate(outs):
            for side in range(2):
                for core in range(2):
                    start, to = row_of(rows, core, distance, side), (2 * side + core) * rows
                    out[to : to + rows, columns] = sums[start : start + rows, :]
        return carry

    lax.fori_loop(0, (part.stop - part.start) // STEP, body, 0)


def forward_distance(toks, weight, part):
    tokens, width = toks.shape
    count = part.stop - part.start
    return call(
        functools.partial(forward_distance_kernel, part),
        "forward_distance",
        [((tokens // N_Y, count), BF16, ON_CHIP)] * N_Y,
        [ON_CHIP, ON_CHIP],
        [toks, weight],
        flops=2 * tokens * width * count,
        size=2 * width * count,
    )


def assemble(grads, pieces, held, core):
    rows = held.shape[0] // (2 * N_Y)
    for grad, piece in zip(grads, pieces):
        for slot, (distance, side) in enumerate(piece):
            start, at = (2 * distance + side) * rows, (2 * slot + core) * rows
            held[start : start + rows, :] = grad[at : at + rows, :]


def times_weight(grad, weight, columns, part):
    return lax.dot_general(
        grad, weight[columns, part], (((1,), (1,)), ((), ())), preferred_element_type=F32
    )


def backward_first_kernel(pieces, part, *refs):
    grads = refs[: len(pieces)]
    weight, out, held = refs[len(pieces) :]
    half = held.shape[0] // 2
    for core in range(2):
        assemble(grads, pieces, held.at[core * half : (core + 1) * half], core)

    def body(i, carry):
        columns = pl.ds(pl.multiple_of(i * STEP, STEP), STEP)
        out[:, columns] = times_weight(held[...], weight, columns, part)
        return carry

    lax.fori_loop(0, weight.shape[0] // STEP, body, 0)


def backward_first(grads, weight, pieces, part):
    width, hidden = weight.shape[0], part.stop - part.start
    count = sum(grad.shape[0] for grad in grads)
    return call(
        functools.partial(backward_first_kernel, pieces, part),
        "backward_first",
        [((count, width), F32, ON_CHIP)],
        [ON_CHIP] * (len(grads) + 1),
        [*grads, weight],
        flops=2 * count * width * hidden,
        size=2 * width * hidden,
        scratch=[pltpu.VMEM((count, hidden), BF16)],
    )[0]


def backward_last_kernel(pieces, part, core, place, *refs):
    grads = refs[: len(pieces)]
    weight, begun, out, held = refs[len(pieces) :]
    assemble(grads, pieces, held, core)
    rows = out.shape[1]
    half = slice(core * 2 * N_Y * rows, (core + 1) * 2 * N_Y * rows)

    def body(i, carry):
        columns = pl.ds(pl.multiple_of(i * STEP, STEP), STEP)
        total = begun[half, columns] + times_weight(held[...], weight, columns, part)
        total = total.astype(BF16)
        for distance in range(N_Y):
            for side in range(2):
                start = (2 * distance + side) * rows
                out[block_of(place, distance, side), :, columns] = total[start : start + rows, :]
        return carry

    lax.fori_loop(0, weight.shape[0] // STEP, body, 0)


def backward_last(place, grads, weight, begun, pieces, part, core, name):
    width, hidden = weight.shape[0], part.stop - part.start
    count = begun.shape[0] // 2
    return call(
        functools.partial(backward_last_kernel, pieces, part, core),
        name,
        [((2 * N_Y, count // (2 * N_Y), width), BF16, ON_CHIP)],
        [SCALARS] + [ON_CHIP] * (len(grads) + 2),
        [place, *grads, weight, begun],
        flops=2 * count * width * hidden,
        size=2 * width * hidden,
        scratch=[pltpu.VMEM((count, hidden), BF16)],
    )[0]


def add_kernel(mine, got, out):
    out[...] = mine[...] + got[...]


def turn_kernel(tok, out, held, sem):
    held[...] = tok[...].T
    copy = pltpu.make_async_copy(held, out, sem)
    copy.start()
    copy.wait()


def turn(tok):
    rows, width = tok.shape
    return call(
        turn_kernel,
        "turn_tokens",
        [((width, rows), BF16, IN_HBM)],
        [ON_CHIP],
        [tok],
        flops=0,
        size=4 * rows * width,
        scratch=[pltpu.VMEM((width, rows), BF16), pltpu.SemaphoreType.DMA(())],
    )[0]


def weight_grad_kernel(pieces, offsets, *refs):
    turned, *grads = refs[: len(pieces) + 1]
    out, held_turned, held, tiles, sems, load_sems = refs[len(pieces) + 1 :]
    step = tiles.shape[2]
    steps = held.shape[1] // step
    rows = held.shape[0] // (4 * N_Y)
    loads = [pltpu.make_async_copy(turned, held_turned, load_sems.at[0])]
    for grad, piece, offset in zip(grads, pieces, offsets):
        columns = slice(offset, offset + grad.shape[1])
        for slot, (distance, side) in enumerate(piece):
            for core in range(2):
                start, at = row_of(rows, core, distance, side), (2 * slot + core) * rows
                loads.append(
                    pltpu.make_async_copy(
                        grad.at[at : at + rows, :],
                        held.at[start : start + rows, columns],
                        load_sems.at[len(loads)],
                    )
                )
    for load in loads:
        load.start()
    for load in loads:
        load.wait()

    def copy(i):
        columns = pl.ds(pl.multiple_of(i * step, step), step)
        slot = lax.rem(i, 2)
        return pltpu.make_async_copy(tiles.at[slot], out.at[:, columns], sems.at[slot])

    def body(i, carry):
        columns = pl.ds(pl.multiple_of(i * step, step), step)

        @pl.when(i >= 2)
        def _():
            copy(i - 2).wait()

        total = jnp.dot(held_turned[...], held[:, columns], preferred_element_type=F32)
        tiles[lax.rem(i, 2)] = total.astype(BF16)
        copy(i).start()
        return carry

    lax.fori_loop(0, steps, body, 0)
    copy(steps - 2).wait()
    copy(steps - 1).wait()


def weight_grad_of(turned, grads, pieces, offsets, hidden):
    width, rows = turned.shape
    return call(
        functools.partial(weight_grad_kernel, pieces, offsets),
        "weight_grad",
        [((width, hidden), BF16, IN_HBM)],
        [ANYWHERE] * (1 + len(grads)),
        [turned, *grads],
        flops=2 * rows * width * hidden,
        size=2 * width * hidden,
        scratch=[
            pltpu.VMEM(turned.shape, BF16),
            pltpu.VMEM((rows, hidden), BF16),
            pltpu.VMEM((2, width, STEP), BF16),
            pltpu.SemaphoreType.DMA((2,)),
            pltpu.SemaphoreType.DMA((1 + 2 * sum(len(piece) for piece in pieces),)),
        ],
        limit=56,
    )[0]


def sum_distance_kernel(mine, got_1, got_2, got_3, near, far):
    rows = near.shape[0]
    for columns in tiles_of(near.shape[1]):
        total = mine[:, columns].astype(F32)
        for got in (got_1, got_2, got_3):
            total += got[:, columns].astype(F32)
        near[:, columns] = total[:rows]
        far[:, columns] = total[rows:].astype(BF16)


def sum_side_kernel(mine, got, *outs):
    rows = outs[0].shape[0] // 2
    for columns in tiles_of(mine.shape[1]):
        for distance, out in enumerate(outs):
            for core in range(2):
                start = (core * N_Y + distance) * rows
                block = slice(start, start + rows)
                total = mine[block, columns].astype(F32) + got[block, columns].astype(F32)
                out[core * rows : (core + 1) * rows, columns] = total.astype(out.dtype)


def gelu_kernel(offset, place, *refs):
    terms = refs[:-3]
    cot, act, grad = refs[-3:]
    rows = act.shape[0] // 2
    for side in range(2):
        core = lax.rem(place[2] + side, 2)
        block = slice(side * rows, (side + 1) * rows)
        absolute = pl.ds(pl.multiple_of(core * rows, rows), rows)
        for columns in tiles_of(act.shape[1]):
            pre = terms[0][block, columns].astype(F32)
            for term in terms[1:]:
                pre += term[block, columns].astype(F32)
            value, slope = gelu_parts(pre)
            act[absolute, columns] = value.astype(BF16)
            from_cot = slice(offset + columns.start, offset + columns.stop)
            grad[block, columns] = (cot[absolute, from_cot].astype(F32) * slope).astype(BF16)


def gelu_step(place, terms, cot, offset, name):
    shape = terms[0].shape
    size = shape[0] * shape[1]
    return call(
        functools.partial(gelu_kernel, offset),
        name,
        [(shape, BF16, ON_CHIP), (shape, BF16, ON_CHIP)],
        [SCALARS] + [ON_CHIP] * (len(terms) + 1),
        [place, *terms, cot],
        flops=40 * size,
        size=8 * size,
        transcendentals=size,
    )


def last_sum_kernel(got, out):
    for columns in tiles_of(out.shape[1]):
        total = got[0, :, columns].astype(F32)
        for i in range(1, got.shape[0]):
            total += got[i, :, columns].astype(F32)
        out[:, columns] = total.astype(BF16)


def local(tokens, weight, cotangent):
    rows, width = tokens.shape
    block, hidden = cotangent.shape
    cut = hidden // 2
    part_a, part_b = slice(0, cut), slice(cut, hidden)
    small_a, small_b = (block, cut), (block, hidden - cut)
    place = jnp.stack([lax.axis_index(a) for a in ("y", "xh", "c")]).astype(jnp.int32)

    spread = jnp.broadcast_to(tokens[None], (8, rows, width))
    own = lax.all_to_all(spread, PLANE, 0, 0, tiled=True)
    other = other_core(own)

    held = load(after(weight, own), part_b, "load_forward")
    toks, *sides = forward_side(place, own, other, held)
    got_side = across(sides[1])
    parts = forward_distance(toks, weight, part_a)
    got_a = [ahead(parts[d], d) for d in (1, 2, 3)]
    got_side = after(got_side, parts[0])
    kept, *sent = call(
        sum_side_kernel,
        "sum_b",
        [(small_b, F32 if d == 0 else BF16, ON_CHIP) for d in range(N_Y)],
        [ON_CHIP] * 2,
        [sides[0], got_side],
        flops=8 * block * hidden,
        size=16 * block * hidden,
    )
    got_b = [ahead(sent[d - 1], d) for d in (1, 2, 3)]
    got_a = after(got_a, sent[0])
    near, far = call(
        sum_distance_kernel,
        "sum_a",
        [(small_a, F32, ON_CHIP), (small_a, BF16, ON_CHIP)],
        [ON_CHIP] * 4,
        [parts[0], *got_a],
        flops=8 * block * hidden,
        size=16 * block * hidden,
    )
    got_far = across(far)

    act_b, grad_b = gelu_step(place, [kept, *got_b], cotangent, cut, "gelu_b")
    got_far = after(got_far, grad_b)
    act_a, grad_a = gelu_step(place, [near, got_far], cotangent, 0, "gelu_a")
    late_b = after(grad_b, grad_a)
    by_y = [grad_b]
    by_y += [ahead(late_b if d == 1 else grad_b, -d) for d in (1, 2, 3)]
    both = jnp.concatenate([grad_a, across(grad_a)], axis=0)
    by_y_far = [across(after(grad, both) if d == 1 else grad) for d, grad in enumerate(by_y)]
    wide = [both] + [ahead(after(both, by_y[2]) if d == 2 else both, -d) for d in (1, 2, 3)]
    turned = turn(after(toks, both))
    activated = jnp.concatenate([act_a, act_b], axis=1)

    grads_b = [*by_y, *by_y_far]
    pieces_b = tuple(((d, s),) for s in range(2) for d in range(N_Y))
    begun = backward_first(after(grads_b, turned, activated), weight, pieces_b, part_b)
    wide_last = after(wide, begun)
    theirs = backward_last(place, wide_last, weight, begun, BY_DISTANCE, part_a, 1, "backward_other")
    arrived = other_core(theirs)
    wide_last = after(wide_last, theirs)
    mine = backward_last(place, wide_last, weight, begun, BY_DISTANCE, part_a, 0, "backward_own")
    (chip,) = call(
        add_kernel,
        "chip_sum",
        [(mine.shape, BF16, ON_CHIP)],
        [ON_CHIP] * 2,
        [mine, arrived],
        flops=mine.size,
        size=6 * mine.size,
    )
    last = lax.all_to_all(chip, PLANE, 0, 0, tiled=True)
    grads = after([*grads_b, *wide], chip)
    offsets = [cut] * len(grads_b) + [0] * len(wide)
    weight_grad = weight_grad_of(turned, grads, pieces_b + BY_DISTANCE, offsets, hidden)
    (input_grad,) = call(
        last_sum_kernel,
        "last_sum",
        [((rows, width), BF16, ON_CHIP)],
        [ON_CHIP],
        [last],
        flops=8 * rows * width,
        size=16 * rows * width,
    )
    return (activated, input_grad, weight_grad)


def solution(mesh):
    fine = Mesh(mesh.devices.reshape(N_Y, 2, 2, 4, 2), ("y", "xh", "xl", "z", "c"))
    col = ("xl", "z", "c")
    return jax.shard_map(
        local,
        mesh=fine,
        in_specs=(P(col, ROW), P(ROW, col), P(ROW, col)),
        out_specs=(P(ROW, col), P(col, ROW), P(ROW, col)),
        check_vma=False,
    )
```
